256 devices in a mesh: member: 32 (over z_hi, x, y), lat: 2 (over core), lon: 4 (over z_lo).
Axes of the slice: x: 4, y: 4, z: 8 (z_hi: 2, z_lo: 4; z = z_hi * 4 + z_lo), core: 2. Of those that a mesh axis runs over, the one named last changes fastest.
Arguments:
- theta: float32 [128, 256, 1536], P('member', 'lat', 'lon'), may hold values from -6 to 6
- tracer: float32 [2, 256, 1536], P(None, 'lat', 'lon'), may hold values from -6 to 6
- velocity: float32 [2, 2, 256, 1536], P(None, None, 'lat', 'lon'), may hold values from -0.2 to 0.2
- obs_index: int32 [6144], P(('lat', 'lon')), may hold values from 0 to 49151
- observed: float32 [6144], P(('lat', 'lon')), may hold values from -6 to 6
- noise_var: float32 [6144], P(('lat', 'lon')), may hold values from 0.1 to 1
- obs_perturb: float32 [6144, 128], P(('lat', 'lon'), 'member'), may hold values from -6 to 6
Outputs:
- theta_new: float32 [128, 256, 1536], P('member', 'lat', 'lon')
- predicted: float32 [6144, 128], P(('lat', 'lon'), 'member')
The draws below stay inside these ranges and needn't reach their ends.
Inputs may be any that keep to these rules, and one draw needn't show every extreme that they name: obs_index[o] is a row-major flat cell index within the 128 x 384 tile of block o // 768, blocks numbered latitude-major; stations may share a cell.
All inputs are finite; a program needn't handle non-finite values.
Results may differ from the reference program's by a relative error of at most 0.0003.
Values sent between devices are 32-bit elements; how exact they have to be, the bound alone decides.
A program may use at most 128 MiB of HBM per device.

```python
import math
import jax
import jax.numpy as jnp
from jax import lax

LAT_DEV = 128
LON_DEV = 384
OBS_DEV = 768
STEPS = 2
LM = 1
MEMBERS = 128
NLAT = 256
NLON = 1536
OBS = 6144
N_LON = 4


def place_ends(result, stream_key, least, largest):
    extent = result.shape
    place = [jax.random.randint(jax.random.fold_in(stream_key, axis), (), 0, extent[axis]) for axis in range(len(extent))]
    result = result.at[tuple(place)].set(least)
    longest = extent.index(max(extent))
    place[longest] = (place[longest] + 1) % extent[longest]
    return result.at[tuple(place)].set(largest)


def block_scale(own_key, shape, shards, least, largest):
    level = 1.0
    for dim, shards_of in shards:
        draws = jax.random.uniform(jax.random.fold_in(jax.random.fold_in(own_key, 6), dim), (shards_of,), jnp.float32, least / len(shards), largest / len(shards))
        level = level * jnp.repeat(jnp.exp(draws), shape[dim] // shards_of).reshape((-1,) + (1,) * (len(shape) - 1 - dim))
    return level


def noise(own_key, extent, deviation, reach, shards=(), kind=jnp.bfloat16):
    loudness = block_scale(own_key, extent, shards, -0.22, 0.18) if shards else 1.0
    drawn = jax.random.normal(own_key, extent, jnp.float32) * deviation * loudness
    return jnp.minimum(jnp.maximum(drawn, -reach), reach).astype(kind)


def setup_inputs(seed: int = 0) -> dict:
    keys = jax.random.split(jax.random.key(seed), 8)
    theta = noise(keys[0], (MEMBERS, NLAT, NLON), 1.5, 6.0, ((0, 32), (1, 2), (2, 4)), jnp.float32)
    tracer = noise(keys[1], (2, NLAT, NLON), 1.0, 6.0, ((1, 2), (2, 4)), jnp.float32)
    velocity = jnp.clip(jax.random.uniform(keys[2], (2, 2, NLAT, NLON), jnp.float32, -0.2, 0.2) * block_scale(keys[2], (2, 2, NLAT, NLON), ((2, 2), (3, 4)), -0.4, 0.0), -0.2, 0.2)
    obs_index = place_ends(jax.random.randint(keys[3], (OBS,), 0, LAT_DEV * LON_DEV), jax.random.fold_in(keys[3], 1), 0, (LAT_DEV * LON_DEV) - 1).astype(jnp.int32)
    observed = noise(keys[4], (OBS,), 1.0, 6.0, ((0, 8),), jnp.float32)
    noise_var = jnp.clip(jnp.exp(math.log(1.0) - 2.3025851 * jax.random.uniform(keys[5], (OBS,), jnp.float32) ** block_scale(keys[5], (OBS,), ((0, 8),), -0.2, 0.2)), 0.1, 1.0)
    obs_perturb = noise(keys[6], (OBS, MEMBERS), 1.0, 6.0, ((0, 8), (1, 32)), jnp.float32)
    return {"theta": theta, "tracer": tracer, "velocity": velocity, "obs_index": obs_index, "observed": observed, "noise_var": noise_var, "obs_perturb": obs_perturb}


def advance(c, kap, velocity):
    u = velocity[0]
    v = velocity[1]
    c_w = jnp.roll(c, 1, axis=-1)
    c_e = jnp.roll(c, -1, axis=-1)
    k_w = jnp.roll(kap, 1, axis=-1)
    k_e = jnp.roll(kap, -1, axis=-1)
    cpad = jnp.pad(c, ((0, 0), (1, 1), (0, 0)))
    kpad = jnp.pad(kap, ((0, 0), (1, 1), (0, 0)))
    c_s = cpad[:, :-2]
    c_n = cpad[:, 2:]
    k_s = kpad[:, :-2]
    k_n = kpad[:, 2:]
    adv = -(jnp.maximum(u, 0.0) * (c - c_w) + jnp.minimum(u, 0.0) * (c_e - c))
    adv = adv - (jnp.maximum(v, 0.0) * (c - c_s) + jnp.minimum(v, 0.0) * (c_n - c))
    diff = 0.5 * ((kap + k_w) * (c_w - c) + (kap + k_e) * (c_e - c) + (kap + k_s) * (c_s - c) + (kap + k_n) * (c_n - c))
    return c + adv + diff + 0.2 * (c[::-1] - c)

def reference(theta, tracer, velocity, obs_index, observed, noise_var, obs_perturb):
    block = jnp.arange(OBS, dtype=jnp.int32) // OBS_DEV
    rows = block // N_LON * LAT_DEV + obs_index // LON_DEV
    cols = block % N_LON * LON_DEV + obs_index % LON_DEV
    flat = (rows * NLON + cols).astype(jnp.int32)

    def forward(one_theta):
        kap = (0.1 * jax.nn.sigmoid(one_theta))[None]
        c = tracer
        for step in range(STEPS):
            c = advance(c, kap, velocity)
        return jnp.take(c[0].reshape(-1), flat)
    predicted = lax.map(forward, theta).T
    scale = 1.0 / jnp.sqrt(jnp.float32(MEMBERS - 1))
    anom_g = (predicted - lax.optimization_barrier(jnp.mean(predicted, axis=1, keepdims=True))) * scale
    weighted = anom_g / noise_var[:, None]
    gram = jnp.dot(weighted.T, anom_g, precision=lax.Precision.HIGHEST)
    innov = observed[:, None] + jnp.sqrt(noise_var)[:, None] * obs_perturb - predicted
    rhs = jnp.dot(weighted.T, innov, precision=lax.Precision.HIGHEST)
    damped = gram + LM * jnp.eye(MEMBERS, dtype=gram.dtype)
    factor = jnp.linalg.cholesky(damped)
    half = lax.linalg.triangular_solve(factor, rhs, left_side=True, lower=True)
    weights = lax.linalg.triangular_solve(factor, half, left_side=True, lower=True, transpose_a=True)
    fields = theta.reshape(MEMBERS, -1)
    anom_t = (fields - lax.optimization_barrier(jnp.mean(fields, axis=0, keepdims=True))) * scale
    update = jnp.dot(weights.T, anom_t, precision=lax.Precision.HIGHEST)
    theta_new = theta + update.reshape(theta.shape)
    return (theta_new, predicted)
```

```python
import functools

import jax
import jax.numpy as jnp
from jax import lax
from jax.experimental import pallas as pl
from jax.experimental.pallas import tpu as pltpu
from jax.sharding import PartitionSpec as P

LM = 1.0
MESH = pl.DeviceIdType.MESH
F32 = jnp.float32
BF16 = jnp.bfloat16
LANE = 128
SUB = 8


def lane_shift(x, by):
    return pltpu.roll(x, by % x.shape[1], axis=1)


def south_of(prev, cur):
    return jnp.concatenate([prev[SUB - 1 :], cur[: SUB - 1]], axis=0)


def north_of(cur, nxt):
    return jnp.concatenate([cur[1:], nxt[:1]], axis=0)


def spd_inverse(a):
    n = a.shape[0]
    row_id = lax.broadcasted_iota(jnp.int32, (n, n), 0)
    lane_id = lax.broadcasted_iota(jnp.int32, (n, n), 1)
    lane_row = lax.broadcasted_iota(jnp.int32, (1, n), 1)

    def block(_, m):
        for c in range(0, SUB, 2):
            col0 = m[:, c : c + 1]
            col1 = m[:, c + 1 : c + 2]
            row0 = m[c : c + 1, :]
            row1 = m[c + 1 : c + 2, :]
            p00 = m[c : c + 1, c : c + 1]
            p01 = m[c : c + 1, c + 1 : c + 2]
            p11 = m[c + 1 : c + 2, c + 1 : c + 2]
            inv = 1.0 / (p00 * p11 - p01 * p01)
            i00 = p11 * inv
            i01 = -p01 * inv
            i11 = p00 * inv
            row0 = jnp.where(lane_row == c, 1.0, jnp.where(lane_row == c + 1, 0.0, row0))
            row1 = jnp.where(lane_row == c, 0.0, jnp.where(lane_row == c + 1, 1.0, row1))
            new0 = i00 * row0 + i01 * row1
            new1 = i01 * row0 + i11 * row1
            pivot_lanes = (lane_id == c) | (lane_id == c + 1)
            rest = jnp.where(pivot_lanes, 0.0, m) - col0 * new0 - col1 * new1
            m = jnp.where(row_id == c, new0, jnp.where(row_id == c + 1, new1, rest))
        m = jnp.concatenate([m[SUB:], m[:SUB]], axis=0)
        return lane_shift(m, -SUB)

    return lax.fori_loop(0, n // SUB, block, a)


def kernel(
    sizes,
    theta_hbm, tracer_hbm, velocity_hbm, obs_index, obs_cell, vecs, perturb,
    out_hbm, pred_out,
    th_own, x, lat_in, east_out, west_out, east_in, west_in,
    base, diffs, faces, c1, cells,
    th_all, e_all, pred_all, pred_mat, weighted, left, g_own, rs_in, ab, upd,
    in_sem, halo_send, halo_recv, th_send, th_recv, e_send, e_recv, p_send, p_recv,
    r_send, r_recv, a_send, a_recv, o_send, o_recv,
):
    n_mem, n_lat, n_lon = sizes
    half = n_mem // 2
    tiles = n_lat * n_lon
    blocks, mem_local, rows, _ = th_own.shape
    planes, pad_rows, pad_cols = x.shape
    cols = blocks * LANE
    members = n_mem * mem_local
    half_members = members // 2
    chunk_rows = rows // half
    n_chunks = pad_rows // SUB
    obs = perturb.shape[1]
    obs_half = obs // 2
    g_rows = g_own.shape[0]
    part = g_rows // tiles
    scale = 1.0 / float(members - 1) ** 0.5

    m = lax.axis_index("member")
    la = lax.axis_index("lat")
    lo = lax.axis_index("lon")
    zh = m // half
    p = m % half
    t = la * n_lon + lo

    def at_member(peer):
        return {"member": peer, "lat": la, "lon": lo}

    def at_tile(peer):
        return {"member": m, "lat": peer // n_lon, "lon": peer % n_lon}

    loads = [
        pltpu.make_async_copy(theta_hbm.at[:, :, pl.ds(b * LANE, LANE)], th_own.at[b], in_sem.at[4 + b])
        for b in range(blocks)
    ] + [
        pltpu.make_async_copy(
            tracer_hbm, x.at[pl.ds(mem_local, 2), pl.ds(SUB, rows), pl.ds(0, cols)], in_sem.at[1]
        ),
        pltpu.make_async_copy(
            velocity_hbm, x.at[pl.ds(mem_local + 2, 4), pl.ds(SUB, rows), pl.ds(0, cols)], in_sem.at[2]
        ),
    ]
    for load in loads:
        load.start()

    barrier = pltpu.get_barrier_semaphore()

    def greet_member(d, _):
        pl.semaphore_signal(barrier, inc=1, device_id=at_member((m + d) % n_mem), device_id_type=MESH)
        return 0

    def greet_tile(d, _):
        pl.semaphore_signal(barrier, inc=1, device_id=at_tile((t + d) % tiles), device_id_type=MESH)
        return 0

    lax.fori_loop(1, n_mem, greet_member, 0)
    lax.fori_loop(1, tiles, greet_tile, 0)

    def row_of(i):
        return jnp.concatenate([vecs[i, b : b + 1, :] for b in range(obs // LANE)], axis=1)

    observed = row_of(0)
    noise = row_of(1)
    inv_noise = 1.0 / noise
    e_own = observed + jnp.sqrt(noise) * perturb[...]
    e_all[p, 0:mem_local, :] = e_own[:, :obs_half]
    e_all[p, mem_local:SUB, :] = e_own[:, obs_half:]

    for load in loads[:blocks]:
        load.wait()

    def make_kappa(i, _):
        r = pl.multiple_of(i * SUB, SUB)
        for j in range(mem_local):
            for b in range(blocks):
                x[j, pl.ds(r + SUB, SUB), pl.ds(b * LANE, LANE)] = 0.1 * jax.nn.sigmoid(
                    th_own[b, j, pl.ds(r, SUB), :]
                )
        return 0

    lax.fori_loop(0, rows // SUB, make_kappa, 0)
    for load in loads[blocks:]:
        load.wait()

    lane8 = lax.broadcasted_iota(jnp.int32, (SUB, LANE), 1)
    sub8 = lax.broadcasted_iota(jnp.int32, (SUB, LANE), 0)

    def pack(i, _):
        r = pl.multiple_of(i * SUB, SUB)
        east = jnp.zeros((SUB, LANE), F32)
        west = jnp.zeros((SUB, LANE), F32)
        for q in range(planes):
            first = x[q, pl.ds(r + SUB, SUB), pl.ds(0, LANE)]
            last = x[q, pl.ds(r + SUB, SUB), pl.ds(cols - LANE, LANE)]
            east = jnp.where((lane8 // 2) == q, lane_shift(first, 2 * q), east)
            west = jnp.where(((LANE - 1 - lane8) // 2) == q, lane_shift(last, -2 * q), west)
        east_out[pl.ds(r, SUB), :] = east
        west_out[pl.ds(r, SUB), :] = west
        return 0

    lax.fori_loop(0, rows // SUB, pack, 0)

    pl.semaphore_wait(barrier, n_mem - 1 + tiles - 1)

    my_edge = pl.multiple_of((1 - la) * (rows - SUB), SUB)
    their_edge = pl.multiple_of(la * (rows + SUB), SUB)
    lo_w = (lo + n_lon - 1) % n_lon
    lo_e = (lo + 1) % n_lon

    def halo(i, src, dst, lat, lon):
        return pltpu.make_async_remote_copy(
            src_ref=src, dst_ref=dst, send_sem=halo_send.at[i], recv_sem=halo_recv.at[i],
            device_id={"member": m, "lat": lat, "lon": lon}, device_id_type=MESH,
        )

    halos = [
        halo(0, east_out, east_in.at[pl.ds(SUB, rows), :], la, lo_w),
        halo(1, west_out, west_in.at[pl.ds(SUB, rows), :], la, lo_e),
        halo(2, east_out.at[pl.ds(my_edge, SUB), :], east_in.at[pl.ds(their_edge, SUB), :], 1 - la, lo_w),
        halo(3, west_out.at[pl.ds(my_edge, SUB), :], west_in.at[pl.ds(their_edge, SUB), :], 1 - la, lo_e),
        halo(4, x.at[:, pl.ds(my_edge + SUB, SUB), pl.ds(0, cols)], lat_in, 1 - la, lo),
    ]
    for copy in halos:
        copy.start()

    def e_copy(d):
        peer = (p + d) % half
        return pltpu.make_async_remote_copy(
            src_ref=e_all.at[p], dst_ref=e_all.at[p], send_sem=e_send.at[peer], recv_sem=e_recv.at[p],
            device_id=at_member(zh * half + peer), device_id_type=MESH,
        )

    def e_arrival(d):
        peer = (p + d) % half
        return pltpu.make_async_remote_copy(
            src_ref=e_all.at[p], dst_ref=e_all.at[peer], send_sem=e_send.at[peer], recv_sem=e_recv.at[peer],
            device_id=at_member(zh * half + peer), device_id_type=MESH,
        )

    def th_copy(d):
        peer = (m + d) % n_mem
        r = pl.multiple_of((peer % half) * chunk_rows, chunk_rows)
        return pltpu.make_async_remote_copy(
            src_ref=th_own.at[:, :, pl.ds(r, chunk_rows), :],
            dst_ref=th_all.at[:, pl.ds(m * mem_local, mem_local)],
            send_sem=th_send.at[peer], recv_sem=th_recv.at[m],
            device_id=at_member(peer), device_id_type=MESH,
        )

    def th_arrival(d):
        peer = (m + d) % n_mem
        return pltpu.make_async_remote_copy(
            src_ref=th_own.at[:, :, pl.ds(0, chunk_rows), :],
            dst_ref=th_all.at[:, pl.ds(peer * mem_local, mem_local)],
            send_sem=th_send.at[peer], recv_sem=th_recv.at[peer],
            device_id=at_member(peer), device_id_type=MESH,
        )

    def start(copy):
        def body(d, _):
            copy(d).start()
            return 0
        return body

    def wait_recv(copy):
        def body(d, _):
            copy(d).wait_recv()
            return 0
        return body

    def wait_send(copy):
        def body(d, _):
            copy(d).wait_send()
            return 0
        return body

    lax.fori_loop(1, half, start(e_copy), 0)
    lax.fori_loop(1, n_mem, start(th_copy), 0)
    own_chunk = pl.multiple_of(p * chunk_rows, chunk_rows)
    own_th = pltpu.make_async_copy(
        th_own.at[:, :, pl.ds(own_chunk, chunk_rows), :],
        th_all.at[:, pl.ds(m * mem_local, mem_local)],
        in_sem.at[3],
    )
    own_th.start()

    for copy in halos:
        copy.wait_recv()

    for q in range(planes):
        block = lat_in[q]
        x[q, 0:SUB, 0:cols] = jnp.where(la == 1, block, 0.0)
        x[q, pad_rows - SUB : pad_rows, 0:cols] = jnp.where(la == 0, block, 0.0)

    def unpack(i, _):
        r = pl.multiple_of(i * SUB, SUB)
        inside = ((i > 0) | (la == 1)) & ((i < n_chunks - 1) | (la == 0))
        east = jnp.where(inside, east_in[pl.ds(r, SUB), :], 0.0)
        west = jnp.where(inside, west_in[pl.ds(r, SUB), :], 0.0)
        for q in range(planes):
            x[q, pl.ds(r, SUB), pl.ds(cols, LANE)] = jnp.where(
                lane8 < LANE // 2, lane_shift(east, -2 * q), lane_shift(west, 2 * q)
            )
        return 0

    lax.fori_loop(0, n_chunks, unpack, 0)

    def shared(i, _):
        r = pl.multiple_of(i * SUB, SUB)
        before = pl.multiple_of(jnp.maximum(i - 1, 0) * SUB, SUB)
        after = pl.multiple_of(jnp.minimum(i + 1, n_chunks - 1) * SUB, SUB)
        cur = [x[mem_local + l, pl.ds(r, SUB), :] for l in range(2)]
        for l in range(2):
            c = cur[l]
            u = x[mem_local + 2 + l, pl.ds(r, SUB), :]
            v = x[mem_local + 4 + l, pl.ds(r, SUB), :]
            d_w = lane_shift(c, 1) - c
            d_e = lane_shift(c, -1) - c
            d_s = south_of(x[mem_local + l, pl.ds(before, SUB), :], c) - c
            d_n = north_of(c, x[mem_local + l, pl.ds(after, SUB), :]) - c
            adv = jnp.maximum(u, 0.0) * d_w - jnp.minimum(u, 0.0) * d_e
            adv = adv + jnp.maximum(v, 0.0) * d_s - jnp.minimum(v, 0.0) * d_n
            base[l, pl.ds(r, SUB), :] = c + adv + 0.2 * (cur[1 - l] - c)
            for k, d in enumerate((d_w, d_e, d_s, d_n)):
                diffs[l, k, pl.ds(r, SUB), :] = d
        return 0

    lax.fori_loop(0, n_chunks, shared, 0)

    def first_step(i, _):
        r = pl.multiple_of(i * SUB, SUB)
        before = pl.multiple_of(jnp.maximum(i - 1, 0) * SUB, SUB)
        after = pl.multiple_of(jnp.minimum(i + 1, n_chunks - 1) * SUB, SUB)
        inside = ((i > 0) | (la == 1)) & ((i < n_chunks - 1) | (la == 0))
        for j in range(mem_local):
            k = x[j, pl.ds(r, SUB), :]
            f_e = 0.5 * (k + lane_shift(k, -1))
            f_w = lane_shift(f_e, 1)
            f_s = 0.5 * (k + south_of(x[j, pl.ds(before, SUB), :], k))
            f_n = 0.5 * (k + north_of(k, x[j, pl.ds(after, SUB), :]))
            for n, f in enumerate((f_w, f_e, f_s, f_n)):
                faces[j, n, pl.ds(r, SUB), :] = f
            for l in range(2):
                c = base[l, pl.ds(r, SUB), :]
                for n, f in enumerate((f_w, f_e, f_s, f_n)):
                    c = c + f * diffs[l, n, pl.ds(r, SUB), :]
                c1[j, l, pl.ds(r, SUB), :] = jnp.where(inside, c, 0.0)
        return 0

    lax.fori_loop(0, n_chunks, first_step, 0)

    flat_cells = cells.reshape(rows * blocks * SUB, LANE)

    def second_step(i, _):
        r = pl.multiple_of(i * SUB, SUB)
        before = pl.multiple_of((i - 1) * SUB, SUB)
        after = pl.multiple_of((i + 1) * SUB, SUB)
        u = x[mem_local + 2, pl.ds(r, SUB), pl.ds(0, cols)]
        v = x[mem_local + 4, pl.ds(r, SUB), pl.ds(0, cols)]
        winds = (jnp.maximum(u, 0.0), -jnp.minimum(u, 0.0), jnp.maximum(v, 0.0), -jnp.minimum(v, 0.0))
        for j in range(mem_local):
            wide = c1[j, 0, pl.ds(r, SUB), :]
            c = wide[:, :cols]
            sides = (
                lane_shift(wide, 1)[:, :cols],
                lane_shift(wide, -1)[:, :cols],
                south_of(c1[j, 0, pl.ds(before, SUB), pl.ds(0, cols)], c),
                north_of(c, c1[j, 0, pl.ds(after, SUB), pl.ds(0, cols)]),
            )
            new = c + 0.2 * (c1[j, 1, pl.ds(r, SUB), pl.ds(0, cols)] - c)
            for n in range(4):
                new = new + (winds[n] + faces[j, n, pl.ds(r, SUB), pl.ds(0, cols)]) * (sides[n] - c)
            for b in range(blocks):
                first = ((i - 1) * SUB * blocks + b) * SUB + j
                piece = new[:, b * LANE : (b + 1) * LANE]
                flat_cells[pl.ds(first, SUB, stride=SUB * blocks), :] = piece
                flat_cells[pl.ds(first + mem_local, SUB, stride=SUB * blocks), :] = piece
        return 0

    lax.fori_loop(1, n_chunks - 1, second_step, 0)

    obs_blocks = obs // LANE
    step_of = 8
    obs_lane = [
        jnp.broadcast_to(obs_cell[b : b + 1, :] & (LANE - 1), (SUB, LANE)) for b in range(obs_blocks)
    ]

    def gather(i, accs):
        accs = list(accs)
        for k in range(step_of):
            s = i * step_of + k
            for b in range(obs_blocks):
                block = lax.shift_right_logical(obs_index[b * LANE + s], LANE.bit_length() - 1)
                got = cells[block]
                got = jnp.take_along_axis(got, obs_lane[b], axis=1, mode="promise_in_bounds")
                h = b // (obs_blocks // 2)
                here = (lane8 == s) & (sub8 // mem_local == h)
                a = b % (obs_blocks // 2)
                accs[a] = jnp.where(here, got, accs[a])
        return tuple(accs)

    accs = lax.fori_loop(
        0, LANE // step_of, gather, tuple(jnp.zeros((SUB, LANE), F32) for _ in range(obs_blocks // 2))
    )
    own_pred = jnp.concatenate(accs, axis=1)
    pred_all[m] = own_pred
    pred_out[:, 0:obs_half] = own_pred[0:mem_local]
    pred_out[:, obs_half:obs] = own_pred[mem_local:SUB]

    def p_copy(d):
        peer = (m + d) % n_mem
        return pltpu.make_async_remote_copy(
            src_ref=pred_all.at[m], dst_ref=pred_all.at[m], send_sem=p_send.at[peer], recv_sem=p_recv.at[m],
            device_id=at_member(peer), device_id_type=MESH,
        )

    def p_arrival(d):
        peer = (m + d) % n_mem
        return pltpu.make_async_remote_copy(
            src_ref=pred_all.at[m], dst_ref=pred_all.at[peer], send_sem=p_send.at[peer], recv_sem=p_recv.at[peer],
            device_id=at_member(peer), device_id_type=MESH,
        )

    lax.fori_loop(1, n_mem, start(p_copy), 0)
    lax.fori_loop(1, half, wait_recv(e_arrival), 0)
    lax.fori_loop(1, n_mem, wait_recv(p_arrival), 0)

    low = lax.broadcasted_iota(jnp.int32, (SUB, obs_half), 0) < mem_local

    def unfold(a, b):
        top = jnp.where(low, a, pltpu.roll(b, mem_local, axis=0))
        bottom = jnp.where(low, pltpu.roll(a, mem_local, axis=0), b)
        return jnp.concatenate([top, bottom], axis=1)

    def collect(i, total):
        both = unfold(pred_all[2 * i], pred_all[2 * i + 1])
        pred_mat[pl.ds(pl.multiple_of(i * SUB, SUB), SUB), :] = both
        return total + both

    total = lax.fori_loop(0, n_mem // 2, collect, jnp.zeros((SUB, obs), F32))
    mean = jnp.sum(total, axis=0, keepdims=True) * (1.0 / members)

    def center(i, _):
        r = pl.multiple_of(i * SUB, SUB)
        anom = (pred_mat[pl.ds(r, SUB), :] - mean) * scale
        left[pl.ds(r, SUB), :] = anom
        weighted[pl.ds(r, SUB), :] = anom * inv_noise
        return 0

    lax.fori_loop(0, members // SUB, center, 0)

    def innovate(i, _):
        r = pl.multiple_of(zh * half_members + i * SUB, SUB)
        e = unfold(e_all[2 * i], e_all[2 * i + 1])
        left[pl.ds(pl.multiple_of(members + i * SUB, SUB), SUB), :] = e - pred_mat[pl.ds(r, SUB), :]
        return 0

    lax.fori_loop(0, half_members // SUB, innovate, 0)

    g_own[...] = lax.dot_general(
        left[...], weighted[...], (((1,), (1,)), ((), ())), precision=lax.Precision.HIGHEST,
        preferred_element_type=F32,
    )

    def r_copy(d):
        peer = (t + d) % tiles
        return pltpu.make_async_remote_copy(
            src_ref=g_own.at[pl.ds(pl.multiple_of(peer * part, SUB), part), :], dst_ref=rs_in.at[t],
            send_sem=r_send.at[peer], recv_sem=r_recv.at[t],
            device_id=at_tile(peer), device_id_type=MESH,
        )

    def r_arrival(d):
        peer = (t + d) % tiles
        return pltpu.make_async_remote_copy(
            src_ref=g_own.at[pl.ds(0, part), :], dst_ref=rs_in.at[peer],
            send_sem=r_send.at[peer], recv_sem=r_recv.at[peer],
            device_id=at_tile(peer), device_id_type=MESH,
        )

    my_part = pl.multiple_of(t * part, SUB)
    lax.fori_loop(1, tiles, start(r_copy), 0)
    rs_in[t] = g_own[pl.ds(my_part, part), :]
    lax.fori_loop(1, tiles, wait_recv(r_arrival), 0)
    total_part = rs_in[0]
    for k in range(1, tiles):
        total_part = total_part + rs_in[k]
    ab[pl.ds(my_part, part), :] = total_part

    def a_copy(d):
        peer = (t + d) % tiles
        mine = ab.at[pl.ds(my_part, part), :]
        return pltpu.make_async_remote_copy(
            src_ref=mine, dst_ref=mine, send_sem=a_send.at[peer], recv_sem=a_recv.at[t],
            device_id=at_tile(peer), device_id_type=MESH,
        )

    def a_arrival(d):
        peer = (t + d) % tiles
        return pltpu.make_async_remote_copy(
            src_ref=ab.at[pl.ds(my_part, part), :],
            dst_ref=ab.at[pl.ds(pl.multiple_of(peer * part, SUB), part), :],
            send_sem=a_send.at[peer], recv_sem=a_recv.at[peer],
            device_id=at_tile(peer), device_id_type=MESH,
        )

    lax.fori_loop(1, tiles, start(a_copy), 0)
    lax.fori_loop(1, tiles, wait_recv(a_arrival), 0)

    eye = lax.broadcasted_iota(jnp.int32, (members, members), 0) == lax.broadcasted_iota(
        jnp.int32, (members, members), 1
    )
    inverse = spd_inverse(ab[0:members, :] + jnp.where(eye, LM, 0.0))
    w = jnp.dot(
        ab[members : members + half_members, :], inverse, precision=lax.Precision.HIGHEST,
        preferred_element_type=F32,
    )
    w = scale * (w - jnp.mean(w, axis=1, keepdims=True))
    w_hi = w.astype(BF16)
    w_lo = (w - w_hi.astype(F32)).astype(BF16)
    lhs = jnp.concatenate(
        [jnp.concatenate([w_hi, w_hi], axis=1), jnp.concatenate([w_lo, jnp.zeros_like(w_lo)], axis=1)], axis=0
    )

    own_th.wait()
    lax.fori_loop(1, n_mem, wait_recv(th_arrival), 0)

    def o_copy(b, d):
        peer = (p + d) % half
        return pltpu.make_async_remote_copy(
            src_ref=upd.at[b, pl.ds(peer * mem_local, mem_local)],
            dst_ref=out_hbm.at[:, pl.ds(own_chunk, chunk_rows), pl.ds(b * LANE, LANE)],
            send_sem=o_send.at[b, peer], recv_sem=o_recv.at[b, p],
            device_id=at_member(zh * half + peer), device_id_type=MESH,
        )

    def o_arrival(b, d):
        peer = (p + d) % half
        return pltpu.make_async_remote_copy(
            src_ref=upd.at[b, pl.ds(peer * mem_local, mem_local)],
            dst_ref=out_hbm.at[
                :, pl.ds(pl.multiple_of(peer * chunk_rows, chunk_rows), chunk_rows), pl.ds(b * LANE, LANE)
            ],
            send_sem=o_send.at[b, peer], recv_sem=o_recv.at[b, peer],
            device_id=at_member(zh * half + peer), device_id_type=MESH,
        )

    flat = th_all.reshape(blocks * members * chunk_rows, LANE)
    upd_flat = upd.reshape(blocks * half_members * chunk_rows, LANE)
    own_out = []
    for b in range(blocks):
        at_b = b * members * chunk_rows
        for r in range(0, chunk_rows, 2):
            field = jnp.concatenate(
                [flat[pl.ds(at_b + r + k, members, stride=chunk_rows), :] for k in range(2)], axis=1
            )
            hi = field.astype(BF16)
            lo_part = (field - hi.astype(F32)).astype(BF16)
            both = jnp.dot(lhs, jnp.concatenate([hi, lo_part], axis=0), preferred_element_type=F32)
            both = both[:half_members] + both[half_members:]
            for k in range(2):
                own = flat[pl.ds(at_b + zh * (half_members * chunk_rows) + r + k, half_members, stride=chunk_rows), :]
                upd_flat[pl.ds(b * half_members * chunk_rows + r + k, half_members, stride=chunk_rows), :] = (
                    own + both[:, k * LANE : (k + 1) * LANE]
                )
        lax.fori_loop(1, half, start(functools.partial(o_copy, b)), 0)
        own_out.append(
            pltpu.make_async_copy(
                upd.at[b, pl.ds(p * mem_local, mem_local)],
                out_hbm.at[:, pl.ds(own_chunk, chunk_rows), pl.ds(b * LANE, LANE)],
                in_sem.at[4 + b],
            )
        )
        own_out[b].start()

    for copy in halos:
        copy.wait_send()
    lax.fori_loop(1, half, wait_send(e_copy), 0)
    lax.fori_loop(1, n_mem, wait_send(th_copy), 0)
    lax.fori_loop(1, n_mem, wait_send(p_copy), 0)
    lax.fori_loop(1, tiles, wait_send(r_copy), 0)
    lax.fori_loop(1, tiles, wait_send(a_copy), 0)
    for b in range(blocks):
        own_out[b].wait()
        lax.fori_loop(1, half, wait_recv(functools.partial(o_arrival, b)), 0)
        lax.fori_loop(1, half, wait_send(functools.partial(o_copy, b)), 0)


def on_device(sizes, theta, tracer, velocity, obs_index, observed, noise_var, obs_perturb):
    n_mem, n_lat, n_lon = sizes
    mem_local, rows, cols = theta.shape
    obs = obs_index.shape[0]
    half = n_mem // 2
    tiles = n_lat * n_lon
    members = n_mem * mem_local
    half_members = members // 2
    chunk_rows = rows // half
    planes = mem_local + 6
    pad_rows, pad_cols = rows + 2 * SUB, cols + LANE
    g_rows = members + half_members
    vecs = jnp.stack([observed.reshape(obs // LANE, LANE), noise_var.reshape(obs // LANE, LANE)])
    dma = pltpu.SemaphoreType.DMA
    theta_new, pred = pl.pallas_call(
        functools.partial(kernel, sizes),
        out_shape=(
            jax.ShapeDtypeStruct(theta.shape, F32),
            jax.ShapeDtypeStruct((mem_local, obs), F32),
        ),
        in_specs=[
            pl.BlockSpec(memory_space=pl.ANY),
            pl.BlockSpec(memory_space=pl.ANY),
            pl.BlockSpec(memory_space=pl.ANY),
            pl.BlockSpec(memory_space=pltpu.SMEM),
            pl.BlockSpec(memory_space=pltpu.VMEM),
            pl.BlockSpec(memory_space=pltpu.VMEM),
            pl.BlockSpec(memory_space=pltpu.VMEM),
        ],
        out_specs=(pl.BlockSpec(memory_space=pl.ANY), pl.BlockSpec(memory_space=pltpu.VMEM)),
        scratch_shapes=[
            pltpu.VMEM((cols // LANE, mem_local, rows, LANE), F32),
            pltpu.VMEM((planes, pad_rows, pad_cols), F32),
            pltpu.VMEM((planes, SUB, cols), F32),
            pltpu.VMEM((rows, LANE), F32),
            pltpu.VMEM((rows, LANE), F32),
            pltpu.VMEM((pad_rows, LANE), F32),
            pltpu.VMEM((pad_rows, LANE), F32),
            pltpu.VMEM((2, pad_rows, pad_cols), F32),
            pltpu.VMEM((2, 4, pad_rows, pad_cols), F32),
            pltpu.VMEM((mem_local, 4, pad_rows, pad_cols), F32),
            pltpu.VMEM((mem_local, 2, pad_rows, pad_cols), F32),
            pltpu.VMEM((rows * (cols // LANE), SUB, LANE), F32),
            pltpu.VMEM((cols // LANE, members, chunk_rows, LANE), F32),
            pltpu.VMEM((half, SUB, obs // 2), F32),
            pltpu.VMEM((n_mem, SUB, obs // 2), F32),
            pltpu.VMEM((members, obs), F32),
            pltpu.VMEM((members, obs), F32),
            pltpu.VMEM((g_rows, obs), F32),
            pltpu.VMEM((g_rows, members), F32),
            pltpu.VMEM((tiles, g_rows // tiles, members), F32),
            pltpu.VMEM((g_rows, members), F32),
            pltpu.VMEM((cols // LANE, half_members, chunk_rows, LANE), F32),
            dma((4 + cols // LANE,)),
            dma((5,)), dma((5,)),
            dma((n_mem,)), dma((n_mem,)),
            dma((half,)), dma((half,)),
            dma((n_mem,)), dma((n_mem,)),
            dma((tiles,)), dma((tiles,)),
            dma((tiles,)), dma((tiles,)),
            dma((cols // LANE, half)), dma((cols // LANE, half)),
        ],
        compiler_params=pltpu.CompilerParams(
            collective_id=0, has_side_effects=True, vmem_limit_bytes=56 * 1024 * 1024
        ),
        name="inversion",
    )(theta, tracer, velocity.reshape(4, rows, cols), obs_index, obs_index.reshape(obs // LANE, LANE), vecs, obs_perturb.T)
    return theta_new, pred.T


def solution(mesh):
    placed = (
        P("member", "lat", "lon"),
        P(None, "lat", "lon"),
        P(None, None, "lat", "lon"),
        P(("lat", "lon")),
        P(("lat", "lon")),
        P(("lat", "lon")),
        P(("lat", "lon"), "member"),
    )
    sizes = (mesh.shape["member"], mesh.shape["lat"], mesh.shape["lon"])
    return jax.shard_map(
        functools.partial(on_device, sizes),
        mesh=mesh,
        in_specs=placed,
        out_specs=(P("member", "lat", "lon"), P(("lat", "lon"), "member")),
        check_vma=False,
    )
```

```python
import functools

import jax
import jax.numpy as jnp
from jax import lax
from jax.experimental import pallas as pl
from jax.experimental.pallas import tpu as pltpu
from jax.sharding import PartitionSpec as P

LM = 1.0
MESH = pl.DeviceIdType.MESH
F32 = jnp.float32
BF16 = jnp.bfloat16
LANE = 128
SUB = 8
FAR = (6, 4, 4, 4, 4, 4, 4, 4)


def lane_shift(x, by):
    return pltpu.roll(x, by % x.shape[1], axis=1)


def south_of(prev, cur):
    return jnp.concatenate([prev[SUB - 1 :], cur[: SUB - 1]], axis=0)


def north_of(cur, nxt):
    return jnp.concatenate([cur[1:], nxt[:1]], axis=0)


def invert(mat):
    n = mat.shape[0]
    shape = (SUB, n)
    row_id = lax.broadcasted_iota(jnp.int32, shape, 0)
    lane_id = lax.broadcasted_iota(jnp.int32, shape, 1)

    def row(x, r):
        return jnp.broadcast_to(x[r : r + 1, :], shape)

    def behind(first, panel):
        lanes = [jnp.full(shape, (first + c) & (n - 1), jnp.int32) for c in range(SUB)]
        rows = [row(panel, c) for c in range(SUB)]
        in_panel = (lane_id >= first) & (lane_id < first + SUB)

        def update(tile):
            parts = [
                jnp.take_along_axis(tile, lanes[c], axis=1, mode="promise_in_bounds") * rows[c] for c in range(SUB)
            ]
            while len(parts) > 1:
                parts = [parts[k] + parts[k + 1] for k in range(0, len(parts), 2)]
            return jnp.where(in_panel, 0.0, tile) - parts[0]

        return update

    def eliminate_panel(b, last):
        first = pl.multiple_of(b * SUB, SUB)
        update = behind(first - SUB, last)
        panel = update(mat[pl.ds(first, SUB), :])
        cols = [
            jnp.take_along_axis(panel, jnp.full(shape, first + c, jnp.int32), axis=1, mode="promise_in_bounds")
            for c in range(SUB)
        ]
        for c in range(0, SUB, 2):
            c0, c1 = cols[c], cols[c + 1]
            p00, p01, p11 = row(c0, c), row(c1, c), row(c1, c + 1)
            inv = 1.0 / (p00 * p11 - p01 * p01)
            i00, i01, i11 = p11 * inv, -p01 * inv, p00 * inv

            def eliminate(r0, r1, rest):
                new0 = i00 * r0 + i01 * r1
                new1 = i01 * r0 + i11 * r1
                rest = rest - c0 * new0 - c1 * new1
                return jnp.where(row_id == c, new0, jnp.where(row_id == c + 1, new1, rest))

            at0, at1 = lane_id == first + c, lane_id == first + c + 1
            for k in range(c + 2, SUB):
                cols[k] = eliminate(row(cols[k], c), row(cols[k], c + 1), cols[k])
            panel = eliminate(
                jnp.where(at0, 1.0, jnp.where(at1, 0.0, row(panel, c))),
                jnp.where(at0, 0.0, jnp.where(at1, 1.0, row(panel, c + 1))),
                jnp.where(at0 | at1, 0.0, panel),
            )
        for i in range(n // SUB):
            tile = mat[i * SUB : (i + 1) * SUB, :]
            mat[i * SUB : (i + 1) * SUB, :] = jnp.where(b - 1 == i, tile, update(tile))
        mat[pl.ds(first, SUB), :] = panel
        return panel

    last = lax.fori_loop(0, n // SUB, eliminate_panel, jnp.zeros(shape, F32))
    update = behind(n - SUB, last)
    for i in range(n // SUB - 1):
        mat[i * SUB : (i + 1) * SUB, :] = update(mat[i * SUB : (i + 1) * SUB, :])


def kernel(
    sizes,
    theta_hbm, tracer_hbm, velocity_hbm, obs_index, obs_cell, observed_in, noise_in, perturb,
    out_hbm, pred_out,
    th_own, x, lat_in, east_out, west_out, east_in, west_in,
    base, diffs, faces, c1, cells,
    th_all, e_all, pred_all, pred_mat, weighted, left, g_own, rs_in, ab, mat, upd,
    in_sem, halo_send, halo_recv, th_send, th_recv, f_send, f_recv, e_send, e_recv, p_send, p_recv,
    r_send, r_recv, a_send, a_recv, o_send, o_recv,
):
    n_mem, n_lat, n_lon = sizes
    half = n_mem // 2
    tiles = n_lat * n_lon
    blocks, mem_local, rows, _ = th_own.shape
    planes, pad_rows, pad_cols = x.shape
    cols = blocks * LANE
    members = n_mem * mem_local
    half_members = members // 2
    chunk_rows = rows // half
    n_chunks = pad_rows // SUB
    obs = perturb.shape[1]
    obs_half = obs // 2
    g_rows = g_own.shape[0]
    part = g_rows // tiles
    scale = 1.0 / float(members - 1) ** 0.5

    m = lax.axis_index("member")
    la = lax.axis_index("lat")
    lo = lax.axis_index("lon")
    zh = lax.shift_right_logical(m, half.bit_length() - 1)
    p = m & (half - 1)
    t = la * n_lon + lo

    def at_member(peer):
        return {"member": peer, "lat": la, "lon": lo}

    def at_tile(peer):
        return {"member": m, "lat": lax.shift_right_logical(peer, n_lon.bit_length() - 1), "lon": peer & (n_lon - 1)}

    loads = [
        pltpu.make_async_copy(theta_hbm.at[:, :, pl.ds(b * LANE, LANE)], th_own.at[b], in_sem.at[4 + b])
        for b in range(blocks)
    ] + [
        pltpu.make_async_copy(
            tracer_hbm, x.at[pl.ds(mem_local, 2), pl.ds(SUB, rows), pl.ds(0, cols)], in_sem.at[1]
        ),
        pltpu.make_async_copy(
            velocity_hbm, x.at[pl.ds(mem_local + 2, 4), pl.ds(SUB, rows), pl.ds(0, cols)], in_sem.at[2]
        ),
    ]
    for load in loads:
        load.start()

    barrier = pltpu.get_barrier_semaphore()

    def greet_member(d, _):
        pl.semaphore_signal(barrier, inc=1, device_id=at_member(m ^ d), device_id_type=MESH)
        return 0

    def greet_tile(d, _):
        pl.semaphore_signal(barrier, inc=1, device_id=at_tile(t ^ d), device_id_type=MESH)
        return 0

    lax.fori_loop(1, n_mem, greet_member, 0)
    lax.fori_loop(1, tiles, greet_tile, 0)

    def row_of(ref):
        return jnp.concatenate([ref[b : b + 1, :] for b in range(obs // LANE)], axis=1)

    observed = row_of(observed_in)
    noise = row_of(noise_in)
    inv_noise = 1.0 / noise
    e_own = observed + jnp.sqrt(noise) * perturb[...]
    e_all[p, 0:mem_local, :] = e_own[:, :obs_half]
    e_all[p, mem_local:SUB, :] = e_own[:, obs_half:]

    for load in loads[:blocks]:
        load.wait()

    def make_kappa(i, _):
        r = pl.multiple_of(i * SUB, SUB)
        for j in range(mem_local):
            for b in range(blocks):
                x[j, pl.ds(r + SUB, SUB), pl.ds(b * LANE, LANE)] = 0.1 * jax.nn.sigmoid(
                    th_own[b, j, pl.ds(r, SUB), :]
                )
        return 0

    lax.fori_loop(0, rows // SUB, make_kappa, 0)
    for load in loads[blocks:]:
        load.wait()

    lane8 = lax.broadcasted_iota(jnp.int32, (SUB, LANE), 1)
    sub8 = lax.broadcasted_iota(jnp.int32, (SUB, LANE), 0)

    def pack(i, _):
        r = pl.multiple_of(i * SUB, SUB)
        east = jnp.zeros((SUB, LANE), F32)
        west = jnp.zeros((SUB, LANE), F32)
        for q in range(planes):
            first = x[q, pl.ds(r + SUB, SUB), pl.ds(0, LANE)]
            last = x[q, pl.ds(r + SUB, SUB), pl.ds(cols - LANE, LANE)]
            east = jnp.where((lane8 // 2) == q, lane_shift(first, 2 * q), east)
            west = jnp.where(((LANE - 1 - lane8) // 2) == q, lane_shift(last, -2 * q), west)
        east_out[pl.ds(r, SUB), :] = east
        west_out[pl.ds(r, SUB), :] = west
        return 0

    lax.fori_loop(0, rows // SUB, pack, 0)

    pl.semaphore_wait(barrier, n_mem - 1 + tiles - 1)

    my_edge = pl.multiple_of((1 - la) * (rows - SUB), SUB)
    their_edge = pl.multiple_of(la * (rows + SUB), SUB)
    lo_w = (lo + n_lon - 1) & (n_lon - 1)
    lo_e = (lo + 1) & (n_lon - 1)

    def halo(i, src, dst, lat, lon):
        return pltpu.make_async_remote_copy(
            src_ref=src, dst_ref=dst, send_sem=halo_send.at[i], recv_sem=halo_recv.at[i],
            device_id={"member": m, "lat": lat, "lon": lon}, device_id_type=MESH,
        )

    halos = [
        halo(0, east_out, east_in.at[pl.ds(SUB, rows), :], la, lo_w),
        halo(1, west_out, west_in.at[pl.ds(SUB, rows), :], la, lo_e),
        halo(2, east_out.at[pl.ds(my_edge, SUB), :], east_in.at[pl.ds(their_edge, SUB), :], 1 - la, lo_w),
        halo(3, west_out.at[pl.ds(my_edge, SUB), :], west_in.at[pl.ds(their_edge, SUB), :], 1 - la, lo_e),
        halo(4, x.at[:, pl.ds(my_edge + SUB, SUB), pl.ds(0, cols)], lat_in, 1 - la, lo),
    ]
    for copy in halos:
        copy.start()

    far = [0]

    def send_far(count):
        lax.fori_loop(far[0], far[0] + count, start(far_copy), 0)
        far[0] += count

    def e_copy(d):
        peer = p ^ d
        return pltpu.make_async_remote_copy(
            src_ref=e_all.at[p], dst_ref=e_all.at[p], send_sem=e_send.at[peer], recv_sem=e_recv.at[p],
            device_id=at_member(zh * half + peer), device_id_type=MESH,
        )

    def e_arrival(d):
        peer = p ^ d
        return pltpu.make_async_remote_copy(
            src_ref=e_all.at[p], dst_ref=e_all.at[peer], send_sem=e_send.at[peer], recv_sem=e_recv.at[peer],
            device_id=at_member(zh * half + peer), device_id_type=MESH,
        )

    def th_copy(d):
        peer = m ^ d
        r = pl.multiple_of((peer & (half - 1)) * chunk_rows, chunk_rows)
        return pltpu.make_async_remote_copy(
            src_ref=th_own.at[:, :, pl.ds(r, chunk_rows), :],
            dst_ref=th_all.at[:, pl.ds(m * mem_local, mem_local)],
            send_sem=th_send.at[peer], recv_sem=th_recv.at[m],
            device_id=at_member(peer), device_id_type=MESH,
        )

    def th_arrival(d):
        peer = m ^ d
        return pltpu.make_async_remote_copy(
            src_ref=th_own.at[:, :, pl.ds(0, chunk_rows), :],
            dst_ref=th_all.at[:, pl.ds(peer * mem_local, mem_local)],
            send_sem=th_send.at[peer], recv_sem=th_recv.at[peer],
            device_id=at_member(peer), device_id_type=MESH,
        )

    def far_copy(i):
        b, d = i // half, half + (i & (half - 1))
        peer = m ^ d
        r = pl.multiple_of((peer & (half - 1)) * chunk_rows, chunk_rows)
        return pltpu.make_async_remote_copy(
            src_ref=th_own.at[b, :, pl.ds(r, chunk_rows), :],
            dst_ref=th_all.at[b, pl.ds(m * mem_local, mem_local)],
            send_sem=f_send.at[i], recv_sem=f_recv.at[i],
            device_id=at_member(peer), device_id_type=MESH,
        )

    def far_arrival(i):
        b, d = i // half, half + (i & (half - 1))
        peer = m ^ d
        return pltpu.make_async_remote_copy(
            src_ref=th_own.at[b, :, pl.ds(0, chunk_rows), :],
            dst_ref=th_all.at[b, pl.ds(peer * mem_local, mem_local)],
            send_sem=f_send.at[i], recv_sem=f_recv.at[i],
            device_id=at_member(peer), device_id_type=MESH,
        )

    def start(copy):
        def body(d, _):
            copy(d).start()
            return 0
        return body

    def wait_recv(copy):
        def body(d, _):
            copy(d).wait_recv()
            return 0
        return body

    def wait_send(copy):
        def body(d, _):
            copy(d).wait_send()
            return 0
        return body

    lax.fori_loop(1, half, start(th_copy), 0)
    own_chunk = pl.multiple_of(p * chunk_rows, chunk_rows)
    own_th = pltpu.make_async_copy(
        th_own.at[:, :, pl.ds(own_chunk, chunk_rows), :],
        th_all.at[:, pl.ds(m * mem_local, mem_local)],
        in_sem.at[3],
    )
    own_th.start()
    send_far(FAR[0])

    for copy in halos:
        copy.wait_recv()
    lax.fori_loop(1, half, start(e_copy), 0)

    send_far(FAR[1])

    for q in range(planes):
        block = lat_in[q]
        x[q, 0:SUB, 0:cols] = jnp.where(la == 1, block, 0.0)
        x[q, pad_rows - SUB : pad_rows, 0:cols] = jnp.where(la == 0, block, 0.0)

    def unpack(i, _):
        r = pl.multiple_of(i * SUB, SUB)
        inside = ((i > 0) | (la == 1)) & ((i < n_chunks - 1) | (la == 0))
        east = jnp.where(inside, east_in[pl.ds(r, SUB), :], 0.0)
        west = jnp.where(inside, west_in[pl.ds(r, SUB), :], 0.0)
        for q in range(planes):
            x[q, pl.ds(r, SUB), pl.ds(cols, LANE)] = jnp.where(
                lane8 < LANE // 2, lane_shift(east, -2 * q), lane_shift(west, 2 * q)
            )
        return 0

    lax.fori_loop(0, n_chunks, unpack, 0)

    def shared(i, _):
        r = pl.multiple_of(i * SUB, SUB)
        before = pl.multiple_of(jnp.maximum(i - 1, 0) * SUB, SUB)
        after = pl.multiple_of(jnp.minimum(i + 1, n_chunks - 1) * SUB, SUB)
        cur = [x[mem_local + l, pl.ds(r, SUB), :] for l in range(2)]
        for l in range(2):
            c = cur[l]
            u = x[mem_local + 2 + l, pl.ds(r, SUB), :]
            v = x[mem_local + 4 + l, pl.ds(r, SUB), :]
            d_w = lane_shift(c, 1) - c
            d_e = lane_shift(c, -1) - c
            d_s = south_of(x[mem_local + l, pl.ds(before, SUB), :], c) - c
            d_n = north_of(c, x[mem_local + l, pl.ds(after, SUB), :]) - c
            adv = jnp.maximum(u, 0.0) * d_w - jnp.minimum(u, 0.0) * d_e
            adv = adv + jnp.maximum(v, 0.0) * d_s - jnp.minimum(v, 0.0) * d_n
            base[l, pl.ds(r, SUB), :] = c + adv + 0.2 * (cur[1 - l] - c)
            for k, d in enumerate((d_w, d_e, d_s, d_n)):
                diffs[l, k, pl.ds(r, SUB), :] = d
        return 0

    lax.fori_loop(0, n_chunks, shared, 0)
    send_far(FAR[2])

    def first_step(i, _):
        r = pl.multiple_of(i * SUB, SUB)
        before = pl.multiple_of(jnp.maximum(i - 1, 0) * SUB, SUB)
        after = pl.multiple_of(jnp.minimum(i + 1, n_chunks - 1) * SUB, SUB)
        inside = ((i > 0) | (la == 1)) & ((i < n_chunks - 1) | (la == 0))
        for j in range(mem_local):
            k = x[j, pl.ds(r, SUB), :]
            f_e = 0.5 * (k + lane_shift(k, -1))
            f_w = lane_shift(f_e, 1)
            f_s = 0.5 * (k + south_of(x[j, pl.ds(before, SUB), :], k))
            f_n = 0.5 * (k + north_of(k, x[j, pl.ds(after, SUB), :]))
            for n, f in enumerate((f_w, f_e, f_s, f_n)):
                faces[j, n, pl.ds(r, SUB), :] = f
            for l in range(2):
                c = base[l, pl.ds(r, SUB), :]
                for n, f in enumerate((f_w, f_e, f_s, f_n)):
                    c = c + f * diffs[l, n, pl.ds(r, SUB), :]
                c1[j, l, pl.ds(r, SUB), :] = jnp.where(inside, c, 0.0)
        return 0

    lax.fori_loop(0, n_chunks, first_step, 0)
    send_far(FAR[3])

    flat_cells = cells.reshape(rows * blocks * SUB, LANE)

    def second_step(i, _):
        r = pl.multiple_of(i * SUB, SUB)
        before = pl.multiple_of((i - 1) * SUB, SUB)
        after = pl.multiple_of((i + 1) * SUB, SUB)
        u = x[mem_local + 2, pl.ds(r, SUB), pl.ds(0, cols)]
        v = x[mem_local + 4, pl.ds(r, SUB), pl.ds(0, cols)]
        winds = (jnp.maximum(u, 0.0), -jnp.minimum(u, 0.0), jnp.maximum(v, 0.0), -jnp.minimum(v, 0.0))
        for j in range(mem_local):
            wide = c1[j, 0, pl.ds(r, SUB), :]
            c = wide[:, :cols]
            sides = (
                lane_shift(wide, 1)[:, :cols],
                lane_shift(wide, -1)[:, :cols],
                south_of(c1[j, 0, pl.ds(before, SUB), pl.ds(0, cols)], c),
                north_of(c, c1[j, 0, pl.ds(after, SUB), pl.ds(0, cols)]),
            )
            new = c + 0.2 * (c1[j, 1, pl.ds(r, SUB), pl.ds(0, cols)] - c)
            for n in range(4):
                new = new + (winds[n] + faces[j, n, pl.ds(r, SUB), pl.ds(0, cols)]) * (sides[n] - c)
            for b in range(blocks):
                first = ((i - 1) * SUB * blocks + b) * SUB + j
                piece = new[:, b * LANE : (b + 1) * LANE]
                flat_cells[pl.ds(first, SUB, stride=SUB * blocks), :] = piece
                flat_cells[pl.ds(first + mem_local, SUB, stride=SUB * blocks), :] = piece
        return 0

    lax.fori_loop(1, n_chunks - 1, second_step, 0)
    send_far(FAR[4])

    obs_blocks = obs // LANE
    step_of = 8
    obs_lane = [
        jnp.broadcast_to(obs_cell[b : b + 1, :] & (LANE - 1), (SUB, LANE)) for b in range(obs_blocks)
    ]

    def gather(i, accs):
        accs = list(accs)
        for k in range(step_of):
            s = i * step_of + k
            for b in range(obs_blocks):
                block = lax.shift_right_logical(obs_index[b * LANE + s], LANE.bit_length() - 1)
                got = cells[block]
                got = jnp.take_along_axis(got, obs_lane[b], axis=1, mode="promise_in_bounds")
                h = b // (obs_blocks // 2)
                here = (lane8 == s) & (sub8 // mem_local == h)
                a = b % (obs_blocks // 2)
                accs[a] = jnp.where(here, got, accs[a])
        return tuple(accs)

    accs = lax.fori_loop(
        0, LANE // step_of, gather, tuple(jnp.zeros((SUB, LANE), F32) for _ in range(obs_blocks // 2))
    )
    own_pred = jnp.concatenate(accs, axis=1)
    pred_all[m] = own_pred
    pred_out[:, 0:obs_half] = own_pred[0:mem_local]
    pred_out[:, obs_half:obs] = own_pred[mem_local:SUB]

    def p_copy(d):
        peer = m ^ d
        return pltpu.make_async_remote_copy(
            src_ref=pred_all.at[m], dst_ref=pred_all.at[m], send_sem=p_send.at[peer], recv_sem=p_recv.at[m],
            device_id=at_member(peer), device_id_type=MESH,
        )

    def p_arrival(d):
        peer = m ^ d
        return pltpu.make_async_remote_copy(
            src_ref=pred_all.at[m], dst_ref=pred_all.at[peer], send_sem=p_send.at[peer], recv_sem=p_recv.at[peer],
            device_id=at_member(peer), device_id_type=MESH,
        )

    def p_relay(d):
        far_slot = m ^ half
        return pltpu.make_async_remote_copy(
            src_ref=pred_all.at[far_slot], dst_ref=pred_all.at[far_slot],
            send_sem=p_send.at[far_slot ^ d], recv_sem=p_recv.at[far_slot],
            device_id=at_member(m ^ d), device_id_type=MESH,
        )

    p_copy(half).start()
    lax.fori_loop(1, half, start(p_copy), 0)
    lax.fori_loop(1, half, wait_recv(e_arrival), 0)
    p_arrival(half).wait_recv()
    lax.fori_loop(1, half, start(p_relay), 0)
    send_far(FAR[5])
    lax.fori_loop(1, half, wait_recv(p_arrival), 0)
    lax.fori_loop(half + 1, n_mem, wait_recv(p_arrival), 0)

    low = lax.broadcasted_iota(jnp.int32, (SUB, obs_half), 0) < mem_local

    def unfold(a, b):
        top = jnp.where(low, a, pltpu.roll(b, mem_local, axis=0))
        bottom = jnp.where(low, pltpu.roll(a, mem_local, axis=0), b)
        return jnp.concatenate([top, bottom], axis=1)

    def collect(i, total):
        both = unfold(pred_all[2 * i], pred_all[2 * i + 1])
        pred_mat[pl.ds(pl.multiple_of(i * SUB, SUB), SUB), :] = both
        return total + both

    total = lax.fori_loop(0, n_mem // 2, collect, jnp.zeros((SUB, obs), F32))
    mean = jnp.sum(total, axis=0, keepdims=True) * (1.0 / members)

    def center(i, _):
        r = pl.multiple_of(i * SUB, SUB)
        anom = (pred_mat[pl.ds(r, SUB), :] - mean) * scale
        left[pl.ds(r, SUB), :] = anom
        weighted[pl.ds(r, SUB), :] = anom * inv_noise
        return 0

    lax.fori_loop(0, members // SUB, center, 0)

    def innovate(i, _):
        r = pl.multiple_of(zh * half_members + i * SUB, SUB)
        e = unfold(e_all[2 * i], e_all[2 * i + 1])
        left[pl.ds(pl.multiple_of(members + i * SUB, SUB), SUB), :] = e - pred_mat[pl.ds(r, SUB), :]
        return 0

    lax.fori_loop(0, half_members // SUB, innovate, 0)

    g_own[...] = lax.dot_general(
        left[...], weighted[...], (((1,), (1,)), ((), ())), precision=lax.Precision.HIGHEST,
        preferred_element_type=F32,
    )

    def r_copy(d):
        peer = t ^ d
        return pltpu.make_async_remote_copy(
            src_ref=g_own.at[pl.ds(pl.multiple_of(peer * part, SUB), part), :], dst_ref=rs_in.at[t],
            send_sem=r_send.at[peer], recv_sem=r_recv.at[t],
            device_id=at_tile(peer), device_id_type=MESH,
        )

    def r_arrival(d):
        peer = t ^ d
        return pltpu.make_async_remote_copy(
            src_ref=g_own.at[pl.ds(0, part), :], dst_ref=rs_in.at[peer],
            send_sem=r_send.at[peer], recv_sem=r_recv.at[peer],
            device_id=at_tile(peer), device_id_type=MESH,
        )

    my_part = pl.multiple_of(t * part, SUB)
    lax.fori_loop(1, tiles, start(r_copy), 0)
    send_far(FAR[6])
    rs_in[t] = g_own[pl.ds(my_part, part), :]
    lax.fori_loop(1, tiles, wait_recv(r_arrival), 0)
    total_part = rs_in[0]
    for k in range(1, tiles):
        total_part = total_part + rs_in[k]
    ab[pl.ds(my_part, part), :] = total_part

    def a_copy(d):
        peer = t ^ d
        mine = ab.at[pl.ds(my_part, part), :]
        return pltpu.make_async_remote_copy(
            src_ref=mine, dst_ref=mine, send_sem=a_send.at[peer], recv_sem=a_recv.at[t],
            device_id=at_tile(peer), device_id_type=MESH,
        )

    def a_arrival(d):
        peer = t ^ d
        return pltpu.make_async_remote_copy(
            src_ref=ab.at[pl.ds(my_part, part), :],
            dst_ref=ab.at[pl.ds(pl.multiple_of(peer * part, SUB), part), :],
            send_sem=a_send.at[peer], recv_sem=a_recv.at[peer],
            device_id=at_tile(peer), device_id_type=MESH,
        )

    lax.fori_loop(1, tiles, start(a_copy), 0)
    send_far(FAR[7])
    lax.fori_loop(1, tiles, wait_recv(a_arrival), 0)

    send_far(blocks * half - far[0])
    eye = lax.broadcasted_iota(jnp.int32, (members, members), 0) == lax.broadcasted_iota(
        jnp.int32, (members, members), 1
    )
    mat[...] = ab[0:members, :] + jnp.where(eye, LM, 0.0)
    invert(mat)
    w = jnp.dot(
        ab[members : members + half_members, :], mat[...], precision=lax.Precision.HIGHEST,
        preferred_element_type=F32,
    )
    w = scale * (w - jnp.mean(w, axis=1, keepdims=True))
    w_hi = w.astype(BF16)
    w_lo = (w - w_hi.astype(F32)).astype(BF16)
    lhs = jnp.concatenate(
        [jnp.concatenate([w_hi, w_hi], axis=1), jnp.concatenate([w_lo, jnp.zeros_like(w_lo)], axis=1)], axis=0
    )

    own_th.wait()
    lax.fori_loop(1, half, wait_recv(th_arrival), 0)


    def o_copy(b, d):
        peer = p ^ d
        return pltpu.make_async_remote_copy(
            src_ref=upd.at[b, pl.ds(peer * mem_local, mem_local)],
            dst_ref=out_hbm.at[:, pl.ds(own_chunk, chunk_rows), pl.ds(b * LANE, LANE)],
            send_sem=o_send.at[b, peer], recv_sem=o_recv.at[b, p],
            device_id=at_member(zh * half + peer), device_id_type=MESH,
        )

    def o_arrival(b, d):
        peer = p ^ d
        return pltpu.make_async_remote_copy(
            src_ref=upd.at[b, pl.ds(peer * mem_local, mem_local)],
            dst_ref=out_hbm.at[
                :, pl.ds(pl.multiple_of(peer * chunk_rows, chunk_rows), chunk_rows), pl.ds(b * LANE, LANE)
            ],
            send_sem=o_send.at[b, peer], recv_sem=o_recv.at[b, peer],
            device_id=at_member(zh * half + peer), device_id_type=MESH,
        )

    flat = th_all.reshape(blocks * members * chunk_rows, LANE)
    upd_flat = upd.reshape(blocks * half_members * chunk_rows, LANE)
    own_out = []
    for b in range(blocks):
        at_b = b * members * chunk_rows
        lax.fori_loop(b * half, (b + 1) * half, wait_recv(far_arrival), 0)
        for r in range(0, chunk_rows, 2):
            field = jnp.concatenate(
                [flat[pl.ds(at_b + r + k, members, stride=chunk_rows), :] for k in range(2)], axis=1
            )
            hi = field.astype(BF16)
            lo_part = (field - hi.astype(F32)).astype(BF16)
            both = jnp.dot(lhs, jnp.concatenate([hi, lo_part], axis=0), preferred_element_type=F32)
            both = both[:half_members] + both[half_members:]
            for k in range(2):
                own = flat[pl.ds(at_b + zh * (half_members * chunk_rows) + r + k, half_members, stride=chunk_rows), :]
                upd_flat[pl.ds(b * half_members * chunk_rows + r + k, half_members, stride=chunk_rows), :] = (
                    own + both[:, k * LANE : (k + 1) * LANE]
                )
        lax.fori_loop(1, half, start(functools.partial(o_copy, b)), 0)
        own_out.append(
            pltpu.make_async_copy(
                upd.at[b, pl.ds(p * mem_local, mem_local)],
                out_hbm.at[:, pl.ds(own_chunk, chunk_rows), pl.ds(b * LANE, LANE)],
                in_sem.at[4 + b],
            )
        )
        own_out[b].start()

    for copy in halos:
        copy.wait_send()
    lax.fori_loop(1, half, wait_send(e_copy), 0)
    lax.fori_loop(1, half, wait_send(th_copy), 0)
    lax.fori_loop(0, blocks * half, wait_send(far_copy), 0)
    lax.fori_loop(1, half + 1, wait_send(p_copy), 0)
    lax.fori_loop(1, half, wait_send(p_relay), 0)
    lax.fori_loop(1, tiles, wait_send(r_copy), 0)
    lax.fori_loop(1, tiles, wait_send(a_copy), 0)
    for b in range(blocks):
        own_out[b].wait()
        lax.fori_loop(1, half, wait_recv(functools.partial(o_arrival, b)), 0)
        lax.fori_loop(1, half, wait_send(functools.partial(o_copy, b)), 0)


def on_device(sizes, theta, tracer, velocity, obs_index, observed, noise_var, obs_perturb):
    n_mem, n_lat, n_lon = sizes
    mem_local, rows, cols = theta.shape
    obs = obs_index.shape[0]
    half = n_mem // 2
    tiles = n_lat * n_lon
    members = n_mem * mem_local
    half_members = members // 2
    chunk_rows = rows // half
    planes = mem_local + 6
    pad_rows, pad_cols = rows + 2 * SUB, cols + LANE
    g_rows = members + half_members
    folded = [a.reshape(obs // LANE, LANE) for a in (obs_index, observed, noise_var)]
    dma = pltpu.SemaphoreType.DMA
    theta_new, pred = pl.pallas_call(
        functools.partial(kernel, sizes),
        out_shape=(
            jax.ShapeDtypeStruct(theta.shape, F32),
            jax.ShapeDtypeStruct((mem_local, obs), F32),
        ),
        in_specs=[
            pl.BlockSpec(memory_space=pl.ANY),
            pl.BlockSpec(memory_space=pl.ANY),
            pl.BlockSpec(memory_space=pl.ANY),
            pl.BlockSpec(memory_space=pltpu.SMEM),
            pl.BlockSpec(memory_space=pltpu.VMEM),
            pl.BlockSpec(memory_space=pltpu.VMEM),
            pl.BlockSpec(memory_space=pltpu.VMEM),
            pl.BlockSpec(memory_space=pltpu.VMEM),
        ],
        out_specs=(pl.BlockSpec(memory_space=pl.ANY), pl.BlockSpec(memory_space=pltpu.VMEM)),
        scratch_shapes=[
            pltpu.VMEM((cols // LANE, mem_local, rows, LANE), F32),
            pltpu.VMEM((planes, pad_rows, pad_cols), F32),
            pltpu.VMEM((planes, SUB, cols), F32),
            pltpu.VMEM((rows, LANE), F32),
            pltpu.VMEM((rows, LANE), F32),
            pltpu.VMEM((pad_rows, LANE), F32),
            pltpu.VMEM((pad_rows, LANE), F32),
            pltpu.VMEM((2, pad_rows, pad_cols), F32),
            pltpu.VMEM((2, 4, pad_rows, pad_cols), F32),
            pltpu.VMEM((mem_local, 4, pad_rows, pad_cols), F32),
            pltpu.VMEM((mem_local, 2, pad_rows, pad_cols), F32),
            pltpu.VMEM((rows * (cols // LANE), SUB, LANE), F32),
            pltpu.VMEM((cols // LANE, members, chunk_rows, LANE), F32),
            pltpu.VMEM((half, SUB, obs // 2), F32),
            pltpu.VMEM((n_mem, SUB, obs // 2), F32),
            pltpu.VMEM((members, obs), F32),
            pltpu.VMEM((members, obs), F32),
            pltpu.VMEM((g_rows, obs), F32),
            pltpu.VMEM((g_rows, members), F32),
            pltpu.VMEM((tiles, g_rows // tiles, members), F32),
            pltpu.VMEM((g_rows, members), F32),
            pltpu.VMEM((members, members), F32),
            pltpu.VMEM((cols // LANE, half_members, chunk_rows, LANE), F32),
            dma((4 + cols // LANE,)),
            dma((5,)), dma((5,)),
            dma((n_mem,)), dma((n_mem,)),
            dma((cols // LANE * half,)), dma((cols // LANE * half,)),
            dma((half,)), dma((half,)),
            dma((n_mem,)), dma((n_mem,)),
            dma((tiles,)), dma((tiles,)),
            dma((tiles,)), dma((tiles,)),
            dma((cols // LANE, half)), dma((cols // LANE, half)),
        ],
        compiler_params=pltpu.CompilerParams(
            collective_id=0, has_side_effects=True, vmem_limit_bytes=56 * 1024 * 1024
        ),
        name="inversion",
    )(theta, tracer, velocity.reshape(4, rows, cols), obs_index, *folded, obs_perturb.T)
    return theta_new, pred.T


def solution(mesh):
    placed = (
        P("member", "lat", "lon"),
        P(None, "lat", "lon"),
        P(None, None, "lat", "lon"),
        P(("lat", "lon")),
        P(("lat", "lon")),
        P(("lat", "lon")),
        P(("lat", "lon"), "member"),
    )
    sizes = (mesh.shape["member"], mesh.shape["lat"], mesh.shape["lon"])
    return jax.shard_map(
        functools.partial(on_device, sizes),
        mesh=mesh,
        in_specs=placed,
        out_specs=(P("member", "lat", "lon"), P(("lat", "lon"), "member")),
        check_vma=False,
    )
```

```python
import functools

import jax
import jax.numpy as jnp
from jax import lax
from jax.experimental import pallas as pl
from jax.experimental.pallas import tpu as pltpu
from jax.sharding import PartitionSpec as P

LM = 1.0
MESH = pl.DeviceIdType.MESH
F32 = jnp.float32
BF16 = jnp.bfloat16
LANE = 128
SUB = 8
FAR = (6, 6, 6, 4, 0, 8, 6, 6)


def lane_shift(x, by):
    return pltpu.roll(x, by % x.shape[1], axis=1)


def south_of(prev, cur):
    return jnp.concatenate([prev[SUB - 1 :], cur[: SUB - 1]], axis=0)


def north_of(cur, nxt):
    return jnp.concatenate([cur[1:], nxt[:1]], axis=0)


def invert(mat):
    n = mat.shape[0]
    shape = (SUB, n)
    row_id = lax.broadcasted_iota(jnp.int32, shape, 0)
    lane_id = lax.broadcasted_iota(jnp.int32, shape, 1)

    def row(x, r):
        return jnp.broadcast_to(x[r : r + 1, :], shape)

    row_all = lax.broadcasted_iota(jnp.int32, (n, n), 0)
    lane_all = lax.broadcasted_iota(jnp.int32, (n, n), 1)

    def spread(old, first, panel):
        wide = jnp.concatenate([panel] * (n // SUB), axis=0)
        wide = jnp.where((row_all >= first) & (row_all < first + SUB), wide, 0.0)
        return jnp.dot(old, wide, precision=lax.Precision.HIGHEST, preferred_element_type=F32)

    def behind(first, panel):
        lanes = [jnp.full(shape, (first + c) & (n - 1), jnp.int32) for c in range(SUB)]
        rows = [row(panel, c) for c in range(SUB)]
        in_panel = (lane_id >= first) & (lane_id < first + SUB)

        def update(tile):
            parts = [
                jnp.take_along_axis(tile, lanes[c], axis=1, mode="promise_in_bounds") * rows[c] for c in range(SUB)
            ]
            while len(parts) > 1:
                parts = [parts[k] + parts[k + 1] for k in range(0, len(parts), 2)]
            return jnp.where(in_panel, 0.0, tile) - parts[0]

        return update

    def eliminate_panel(b, last):
        first = pl.multiple_of(b * SUB, SUB)
        update = behind(first - SUB, last)
        panel = update(mat[pl.ds(first, SUB), :])
        cols = [
            jnp.take_along_axis(panel, jnp.full(shape, first + c, jnp.int32), axis=1, mode="promise_in_bounds")
            for c in range(SUB)
        ]
        for c in range(0, SUB, 2):
            c0, c1 = cols[c], cols[c + 1]
            p00, p01, p11 = row(c0, c), row(c1, c), row(c1, c + 1)
            inv = 1.0 / (p00 * p11 - p01 * p01)
            i00, i01, i11 = p11 * inv, -p01 * inv, p00 * inv

            def eliminate(r0, r1, rest):
                new0 = i00 * r0 + i01 * r1
                new1 = i01 * r0 + i11 * r1
                rest = rest - c0 * new0 - c1 * new1
                return jnp.where(row_id == c, new0, jnp.where(row_id == c + 1, new1, rest))

            at0, at1 = lane_id == first + c, lane_id == first + c + 1
            for k in range(c + 2, SUB):
                cols[k] = eliminate(row(cols[k], c), row(cols[k], c + 1), cols[k])
            panel = eliminate(
                jnp.where(at0, 1.0, jnp.where(at1, 0.0, row(panel, c))),
                jnp.where(at0, 0.0, jnp.where(at1, 1.0, row(panel, c + 1))),
                jnp.where(at0 | at1, 0.0, panel),
            )
        old = mat[...]
        kept = (row_all >= first - SUB) & (row_all < first)
        left = (lane_all >= first - SUB) & (lane_all < first)
        mat[...] = jnp.where(kept, old, jnp.where(left, 0.0, old) - spread(old, first - SUB, last))
        mat[pl.ds(first, SUB), :] = panel
        return panel

    last = lax.fori_loop(0, n // SUB, eliminate_panel, jnp.zeros(shape, F32))
    old = mat[...]
    done = jnp.where(lane_all >= n - SUB, 0.0, old) - spread(old, n - SUB, last)
    mat[...] = jnp.where(row_all >= n - SUB, old, done)


def kernel(
    sizes,
    theta_hbm, tracer_hbm, velocity_hbm, obs_index, obs_cell, observed_in, noise_in, perturb,
    out_hbm, pred_out,
    th_own, x, lat_in, east_out, west_out, east_in, west_in,
    base, diffs, faces, c1, cells,
    th_all, e_all, pred_all, pred_mat, weighted, left, g_own, rs_in, ab, mat, upd,
    in_sem, halo_send, halo_recv, th_send, th_recv, f_send, f_recv, e_send, e_recv, p_send, p_recv,
    r_send, r_recv, a_send, a_recv, o_send, o_recv,
):
    n_mem, n_lat, n_lon = sizes
    half = n_mem // 2
    tiles = n_lat * n_lon
    blocks, mem_local, rows, _ = th_own.shape
    planes, pad_rows, pad_cols = x.shape
    cols = blocks * LANE
    members = n_mem * mem_local
    half_members = members // 2
    chunk_rows = rows // half
    n_chunks = pad_rows // SUB
    obs = perturb.shape[1]
    obs_half = obs // 2
    g_rows = g_own.shape[0]
    part = g_rows // half
    scale = 1.0 / float(members - 1) ** 0.5

    m = lax.axis_index("member")
    la = lax.axis_index("lat")
    lo = lax.axis_index("lon")
    zh = lax.shift_right_logical(m, half.bit_length() - 1)
    p = m & (half - 1)
    t = la * n_lon + lo

    def at_member(peer):
        return {"member": peer, "lat": la, "lon": lo}

    def at_tile(peer):
        return {"member": m, "lat": lax.shift_right_logical(peer, n_lon.bit_length() - 1), "lon": peer & (n_lon - 1)}

    loads = [
        pltpu.make_async_copy(theta_hbm.at[:, :, pl.ds(b * LANE, LANE)], th_own.at[b], in_sem.at[4 + b])
        for b in range(blocks)
    ] + [
        pltpu.make_async_copy(
            tracer_hbm, x.at[pl.ds(mem_local, 2), pl.ds(SUB, rows), pl.ds(0, cols)], in_sem.at[1]
        ),
        pltpu.make_async_copy(
            velocity_hbm, x.at[pl.ds(mem_local + 2, 4), pl.ds(SUB, rows), pl.ds(0, cols)], in_sem.at[2]
        ),
    ]
    for load in loads:
        load.start()

    barrier = pltpu.get_barrier_semaphore()

    def greet_member(d, _):
        pl.semaphore_signal(barrier, inc=1, device_id=at_member(m ^ d), device_id_type=MESH)
        return 0

    def greet_tile(d, _):
        pl.semaphore_signal(barrier, inc=1, device_id=at_tile(t ^ d), device_id_type=MESH)
        return 0

    lax.fori_loop(1, n_mem, greet_member, 0)
    lax.fori_loop(1, tiles, greet_tile, 0)

    def row_of(ref):
        return jnp.concatenate([ref[b : b + 1, :] for b in range(obs // LANE)], axis=1)

    observed = row_of(observed_in)
    noise = row_of(noise_in)
    inv_noise = 1.0 / noise
    e_own = observed + jnp.sqrt(noise) * perturb[...]
    e_all[p, 0:mem_local, :] = e_own[:, :obs_half]
    e_all[p, mem_local:SUB, :] = e_own[:, obs_half:]

    for load in loads[:blocks]:
        load.wait()

    def make_kappa(i, _):
        r = pl.multiple_of(i * SUB, SUB)
        for j in range(mem_local):
            for b in range(blocks):
                x[j, pl.ds(r + SUB, SUB), pl.ds(b * LANE, LANE)] = 0.1 * jax.nn.sigmoid(
                    th_own[b, j, pl.ds(r, SUB), :]
                )
        return 0

    lax.fori_loop(0, rows // SUB, make_kappa, 0)
    for load in loads[blocks:]:
        load.wait()

    lane8 = lax.broadcasted_iota(jnp.int32, (SUB, LANE), 1)
    sub8 = lax.broadcasted_iota(jnp.int32, (SUB, LANE), 0)

    def pack(i, _):
        r = pl.multiple_of(i * SUB, SUB)
        east = jnp.zeros((SUB, LANE), F32)
        west = jnp.zeros((SUB, LANE), F32)
        for q in range(planes):
            first = x[q, pl.ds(r + SUB, SUB), pl.ds(0, LANE)]
            last = x[q, pl.ds(r + SUB, SUB), pl.ds(cols - LANE, LANE)]
            east = jnp.where((lane8 // 2) == q, lane_shift(first, 2 * q), east)
            west = jnp.where(((LANE - 1 - lane8) // 2) == q, lane_shift(last, -2 * q), west)
        east_out[pl.ds(r, SUB), :] = east
        west_out[pl.ds(r, SUB), :] = west
        return 0

    lax.fori_loop(0, rows // SUB, pack, 0)

    pl.semaphore_wait(barrier, n_mem - 1 + tiles - 1)

    my_edge = pl.multiple_of((1 - la) * (rows - SUB), SUB)
    their_edge = pl.multiple_of(la * (rows + SUB), SUB)
    lo_w = (lo + n_lon - 1) & (n_lon - 1)
    lo_e = (lo + 1) & (n_lon - 1)

    def halo(i, src, dst, lat, lon):
        return pltpu.make_async_remote_copy(
            src_ref=src, dst_ref=dst, send_sem=halo_send.at[i], recv_sem=halo_recv.at[i],
            device_id={"member": m, "lat": lat, "lon": lon}, device_id_type=MESH,
        )

    halos = [
        halo(0, east_out, east_in.at[pl.ds(SUB, rows), :], la, lo_w),
        halo(1, west_out, west_in.at[pl.ds(SUB, rows), :], la, lo_e),
        halo(2, east_out.at[pl.ds(my_edge, SUB), :], east_in.at[pl.ds(their_edge, SUB), :], 1 - la, lo_w),
        halo(3, west_out.at[pl.ds(my_edge, SUB), :], west_in.at[pl.ds(their_edge, SUB), :], 1 - la, lo_e),
        halo(4, x.at[:, pl.ds(my_edge + SUB, SUB), pl.ds(0, cols)], lat_in, 1 - la, lo),
    ]
    for copy in halos:
        copy.start()

    far = [0]

    def send_far(count):
        lax.fori_loop(far[0], far[0] + count, start(far_copy), 0)
        far[0] += count

    def e_copy(d):
        peer = p ^ d
        return pltpu.make_async_remote_copy(
            src_ref=e_all.at[p], dst_ref=e_all.at[p], send_sem=e_send.at[peer], recv_sem=e_recv.at[p],
            device_id=at_member(zh * half + peer), device_id_type=MESH,
        )

    def e_arrival(d):
        peer = p ^ d
        return pltpu.make_async_remote_copy(
            src_ref=e_all.at[p], dst_ref=e_all.at[peer], send_sem=e_send.at[peer], recv_sem=e_recv.at[peer],
            device_id=at_member(zh * half + peer), device_id_type=MESH,
        )

    def th_copy(d):
        peer = m ^ d
        r = pl.multiple_of((peer & (half - 1)) * chunk_rows, chunk_rows)
        return pltpu.make_async_remote_copy(
            src_ref=th_own.at[:, :, pl.ds(r, chunk_rows), :],
            dst_ref=th_all.at[:, pl.ds(m * mem_local, mem_local)],
            send_sem=th_send.at[peer], recv_sem=th_recv.at[m],
            device_id=at_member(peer), device_id_type=MESH,
        )

    def th_arrival(d):
        peer = m ^ d
        return pltpu.make_async_remote_copy(
            src_ref=th_own.at[:, :, pl.ds(0, chunk_rows), :],
            dst_ref=th_all.at[:, pl.ds(peer * mem_local, mem_local)],
            send_sem=th_send.at[peer], recv_sem=th_recv.at[peer],
            device_id=at_member(peer), device_id_type=MESH,
        )

    def far_copy(i):
        b, d = i // half, half + (i & (half - 1))
        peer = m ^ d
        r = pl.multiple_of((peer & (half - 1)) * chunk_rows, chunk_rows)
        return pltpu.make_async_remote_copy(
            src_ref=th_own.at[b, :, pl.ds(r, chunk_rows), :],
            dst_ref=th_all.at[b, pl.ds(m * mem_local, mem_local)],
            send_sem=f_send.at[i], recv_sem=f_recv.at[i],
            device_id=at_member(peer), device_id_type=MESH,
        )

    def far_arrival(i):
        b, d = i // half, half + (i & (half - 1))
        peer = m ^ d
        return pltpu.make_async_remote_copy(
            src_ref=th_own.at[b, :, pl.ds(0, chunk_rows), :],
            dst_ref=th_all.at[b, pl.ds(peer * mem_local, mem_local)],
            send_sem=f_send.at[i], recv_sem=f_recv.at[i],
            device_id=at_member(peer), device_id_type=MESH,
        )

    def start(copy):
        def body(d, _):
            copy(d).start()
            return 0
        return body

    def wait_recv(copy):
        def body(d, _):
            copy(d).wait_recv()
            return 0
        return body

    def wait_send(copy):
        def body(d, _):
            copy(d).wait_send()
            return 0
        return body

    lax.fori_loop(1, half, start(th_copy), 0)
    own_chunk = pl.multiple_of(p * chunk_rows, chunk_rows)
    own_th = pltpu.make_async_copy(
        th_own.at[:, :, pl.ds(own_chunk, chunk_rows), :],
        th_all.at[:, pl.ds(m * mem_local, mem_local)],
        in_sem.at[3],
    )
    own_th.start()
    send_far(FAR[0])

    for copy in halos:
        copy.wait_recv()
    lax.fori_loop(1, half, start(e_copy), 0)

    send_far(FAR[1])

    for q in range(planes):
        block = lat_in[q]
        x[q, 0:SUB, 0:cols] = jnp.where(la == 1, block, 0.0)
        x[q, pad_rows - SUB : pad_rows, 0:cols] = jnp.where(la == 0, block, 0.0)

    def unpack(i, _):
        r = pl.multiple_of(i * SUB, SUB)
        inside = ((i > 0) | (la == 1)) & ((i < n_chunks - 1) | (la == 0))
        east = jnp.where(inside, east_in[pl.ds(r, SUB), :], 0.0)
        west = jnp.where(inside, west_in[pl.ds(r, SUB), :], 0.0)
        for q in range(planes):
            x[q, pl.ds(r, SUB), pl.ds(cols, LANE)] = jnp.where(
                lane8 < LANE // 2, lane_shift(east, -2 * q), lane_shift(west, 2 * q)
            )
        return 0

    lax.fori_loop(0, n_chunks, unpack, 0)

    def shared(i, _):
        r = pl.multiple_of(i * SUB, SUB)
        before = pl.multiple_of(jnp.maximum(i - 1, 0) * SUB, SUB)
        after = pl.multiple_of(jnp.minimum(i + 1, n_chunks - 1) * SUB, SUB)
        cur = [x[mem_local + l, pl.ds(r, SUB), :] for l in range(2)]
        for l in range(2):
            c = cur[l]
            u = x[mem_local + 2 + l, pl.ds(r, SUB), :]
            v = x[mem_local + 4 + l, pl.ds(r, SUB), :]
            d_w = lane_shift(c, 1) - c
            d_e = lane_shift(c, -1) - c
            d_s = south_of(x[mem_local + l, pl.ds(before, SUB), :], c) - c
            d_n = north_of(c, x[mem_local + l, pl.ds(after, SUB), :]) - c
            adv = jnp.maximum(u, 0.0) * d_w - jnp.minimum(u, 0.0) * d_e
            adv = adv + jnp.maximum(v, 0.0) * d_s - jnp.minimum(v, 0.0) * d_n
            base[l, pl.ds(r, SUB), :] = c + adv + 0.2 * (cur[1 - l] - c)
            for k, d in enumerate((d_w, d_e, d_s, d_n)):
                diffs[l, k, pl.ds(r, SUB), :] = d
        return 0

    lax.fori_loop(0, n_chunks, shared, 0)
    send_far(FAR[2])

    def first_step(i, _):
        r = pl.multiple_of(i * SUB, SUB)
        before = pl.multiple_of(jnp.maximum(i - 1, 0) * SUB, SUB)
        after = pl.multiple_of(jnp.minimum(i + 1, n_chunks - 1) * SUB, SUB)
        inside = ((i > 0) | (la == 1)) & ((i < n_chunks - 1) | (la == 0))
        for j in range(mem_local):
            k = x[j, pl.ds(r, SUB), :]
            f_e = 0.5 * (k + lane_shift(k, -1))
            f_w = lane_shift(f_e, 1)
            f_s = 0.5 * (k + south_of(x[j, pl.ds(before, SUB), :], k))
            f_n = 0.5 * (k + north_of(k, x[j, pl.ds(after, SUB), :]))
            for n, f in enumerate((f_w, f_e, f_s, f_n)):
                faces[j, n, pl.ds(r, SUB), :] = f
            for l in range(2):
                c = base[l, pl.ds(r, SUB), :]
                for n, f in enumerate((f_w, f_e, f_s, f_n)):
                    c = c + f * diffs[l, n, pl.ds(r, SUB), :]
                c1[j, l, pl.ds(r, SUB), :] = jnp.where(inside, c, 0.0)
        return 0

    lax.fori_loop(0, n_chunks, first_step, 0)
    send_far(FAR[3])

    flat_cells = cells.reshape(rows * blocks * SUB, LANE)

    def second_step(i, _):
        r = pl.multiple_of(i * SUB, SUB)
        before = pl.multiple_of((i - 1) * SUB, SUB)
        after = pl.multiple_of((i + 1) * SUB, SUB)
        u = x[mem_local + 2, pl.ds(r, SUB), pl.ds(0, cols)]
        v = x[mem_local + 4, pl.ds(r, SUB), pl.ds(0, cols)]
        winds = (jnp.maximum(u, 0.0), -jnp.minimum(u, 0.0), jnp.maximum(v, 0.0), -jnp.minimum(v, 0.0))
        for j in range(mem_local):
            wide = c1[j, 0, pl.ds(r, SUB), :]
            c = wide[:, :cols]
            sides = (
                lane_shift(wide, 1)[:, :cols],
                lane_shift(wide, -1)[:, :cols],
                south_of(c1[j, 0, pl.ds(before, SUB), pl.ds(0, cols)], c),
                north_of(c, c1[j, 0, pl.ds(after, SUB), pl.ds(0, cols)]),
            )
            new = c + 0.2 * (c1[j, 1, pl.ds(r, SUB), pl.ds(0, cols)] - c)
            for n in range(4):
                new = new + (winds[n] + faces[j, n, pl.ds(r, SUB), pl.ds(0, cols)]) * (sides[n] - c)
            for b in range(blocks):
                first = ((i - 1) * SUB * blocks + b) * SUB + j
                piece = new[:, b * LANE : (b + 1) * LANE]
                flat_cells[pl.ds(first, SUB, stride=SUB * blocks), :] = piece
                flat_cells[pl.ds(first + mem_local, SUB, stride=SUB * blocks), :] = piece
        return 0

    lax.fori_loop(1, n_chunks - 1, second_step, 0)
    send_far(FAR[4])

    obs_blocks = obs // LANE
    step_of = 8
    low8 = sub8 < mem_local
    obs_lane = [
        jnp.where(
            low8,
            jnp.broadcast_to(obs_cell[a : a + 1, :], (SUB, LANE)),
            jnp.broadcast_to(obs_cell[a + obs_blocks // 2 : a + obs_blocks // 2 + 1, :], (SUB, LANE)),
        )
        & (LANE - 1)
        for a in range(obs_blocks // 2)
    ]

    def gather(i, accs):
        accs = list(accs)
        for k in range(step_of):
            s = i * step_of + k
            here = lane8 == s
            for a in range(obs_blocks // 2):
                got = [
                    cells[lax.shift_right_logical(obs_index[b * LANE + s], LANE.bit_length() - 1)]
                    for b in (a, a + obs_blocks // 2)
                ]
                got = jnp.where(low8, got[0], got[1])
                got = jnp.take_along_axis(got, obs_lane[a], axis=1, mode="promise_in_bounds")
                accs[a] = jnp.where(here, got, accs[a])
        return tuple(accs)

    accs = lax.fori_loop(
        0, LANE // step_of, gather, tuple(jnp.zeros((SUB, LANE), F32) for _ in range(obs_blocks // 2))
    )
    own_pred = jnp.concatenate(accs, axis=1)
    pred_all[m] = own_pred
    pred_out[:, 0:obs_half] = own_pred[0:mem_local]
    pred_out[:, obs_half:obs] = own_pred[mem_local:SUB]

    def p_copy(d):
        peer = m ^ d
        return pltpu.make_async_remote_copy(
            src_ref=pred_all.at[m], dst_ref=pred_all.at[m], send_sem=p_send.at[peer], recv_sem=p_recv.at[m],
            device_id=at_member(peer), device_id_type=MESH,
        )

    def p_arrival(d):
        peer = m ^ d
        return pltpu.make_async_remote_copy(
            src_ref=pred_all.at[m], dst_ref=pred_all.at[peer], send_sem=p_send.at[peer], recv_sem=p_recv.at[peer],
            device_id=at_member(peer), device_id_type=MESH,
        )

    def p_relay(d):
        far_slot = m ^ half
        return pltpu.make_async_remote_copy(
            src_ref=pred_all.at[far_slot], dst_ref=pred_all.at[far_slot],
            send_sem=p_send.at[far_slot ^ d], recv_sem=p_recv.at[far_slot],
            device_id=at_member(m ^ d), device_id_type=MESH,
        )

    p_copy(half).start()
    lax.fori_loop(1, half, start(p_copy), 0)
    send_far(FAR[5])
    lax.fori_loop(1, half, wait_recv(e_arrival), 0)
    p_arrival(half).wait_recv()
    lax.fori_loop(1, half, start(p_relay), 0)
    lax.fori_loop(1, half, wait_recv(p_arrival), 0)
    lax.fori_loop(half + 1, n_mem, wait_recv(p_arrival), 0)

    low = lax.broadcasted_iota(jnp.int32, (SUB, obs_half), 0) < mem_local

    def unfold(a, b):
        top = jnp.where(low, a, pltpu.roll(b, mem_local, axis=0))
        bottom = jnp.where(low, pltpu.roll(a, mem_local, axis=0), b)
        return jnp.concatenate([top, bottom], axis=1)

    def collect(i, total):
        both = unfold(pred_all[2 * i], pred_all[2 * i + 1])
        pred_mat[pl.ds(pl.multiple_of(i * SUB, SUB), SUB), :] = both
        return total + both

    total = lax.fori_loop(0, n_mem // 2, collect, jnp.zeros((SUB, obs), F32))
    mean = jnp.sum(total, axis=0, keepdims=True) * (1.0 / members)

    def center(i, _):
        r = pl.multiple_of(i * SUB, SUB)
        anom = (pred_mat[pl.ds(r, SUB), :] - mean) * scale
        left[pl.ds(r, SUB), :] = anom
        weighted[pl.ds(r, SUB), :] = anom * inv_noise
        return 0

    lax.fori_loop(0, members // SUB, center, 0)

    def innovate(i, _):
        r = pl.multiple_of(zh * half_members + i * SUB, SUB)
        e = unfold(e_all[2 * i], e_all[2 * i + 1])
        left[pl.ds(pl.multiple_of(members + i * SUB, SUB), SUB), :] = e - pred_mat[pl.ds(r, SUB), :]
        return 0

    lax.fori_loop(0, half_members // SUB, innovate, 0)

    g_own[members + half_members :, :] = jnp.zeros((g_rows - members - half_members, members), F32)
    g_own[0 : members + half_members, :] = lax.dot_general(
        left[...], weighted[...], (((1,), (1,)), ((), ())), precision=lax.Precision.HIGHEST,
        preferred_element_type=F32,
    )

    my_part = pl.multiple_of(p * part, SUB)

    def r_copy(d):
        peer = t ^ d
        return pltpu.make_async_remote_copy(
            src_ref=g_own.at[pl.ds(my_part, part), :], dst_ref=rs_in.at[t],
            send_sem=r_send.at[peer], recv_sem=r_recv.at[t],
            device_id=at_tile(peer), device_id_type=MESH,
        )

    def r_arrival(d):
        peer = t ^ d
        return pltpu.make_async_remote_copy(
            src_ref=g_own.at[pl.ds(0, part), :], dst_ref=rs_in.at[peer],
            send_sem=r_send.at[peer], recv_sem=r_recv.at[peer],
            device_id=at_tile(peer), device_id_type=MESH,
        )

    lax.fori_loop(1, tiles, start(r_copy), 0)
    send_far(FAR[6])
    rs_in[t] = g_own[pl.ds(my_part, part), :]
    lax.fori_loop(1, tiles, wait_recv(r_arrival), 0)
    total_part = rs_in[0]
    for k in range(1, tiles):
        total_part = total_part + rs_in[k]
    ab[pl.ds(my_part, part), :] = total_part

    def a_copy(d):
        peer = p ^ d
        mine = ab.at[pl.ds(my_part, part), :]
        return pltpu.make_async_remote_copy(
            src_ref=mine, dst_ref=mine, send_sem=a_send.at[peer], recv_sem=a_recv.at[p],
            device_id=at_member(zh * half + peer), device_id_type=MESH,
        )

    def a_arrival(d):
        peer = p ^ d
        return pltpu.make_async_remote_copy(
            src_ref=ab.at[pl.ds(my_part, part), :],
            dst_ref=ab.at[pl.ds(pl.multiple_of(peer * part, SUB), part), :],
            send_sem=a_send.at[peer], recv_sem=a_recv.at[peer],
            device_id=at_member(zh * half + peer), device_id_type=MESH,
        )

    lax.fori_loop(1, half, start(a_copy), 0)
    send_far(FAR[7])
    lax.fori_loop(1, half, wait_recv(a_arrival), 0)

    send_far(blocks * half - far[0])
    eye = lax.broadcasted_iota(jnp.int32, (members, members), 0) == lax.broadcasted_iota(
        jnp.int32, (members, members), 1
    )
    mat[...] = ab[0:members, :] + jnp.where(eye, LM, 0.0)
    invert(mat)
    w = jnp.dot(
        ab[members : members + half_members, :], mat[...], precision=lax.Precision.HIGHEST,
        preferred_element_type=F32,
    )
    w = scale * (w - jnp.mean(w, axis=1, keepdims=True))
    w_hi = w.astype(BF16)
    w_lo = (w - w_hi.astype(F32)).astype(BF16)
    lhs = jnp.concatenate(
        [jnp.concatenate([w_hi, w_hi], axis=1), jnp.concatenate([w_lo, jnp.zeros_like(w_lo)], axis=1)], axis=0
    )

    own_th.wait()
    lax.fori_loop(1, half, wait_recv(th_arrival), 0)


    def o_copy(b, d):
        peer = p ^ d
        return pltpu.make_async_remote_copy(
            src_ref=upd.at[b, pl.ds(peer * mem_local, mem_local)],
            dst_ref=out_hbm.at[:, pl.ds(own_chunk, chunk_rows), pl.ds(b * LANE, LANE)],
            send_sem=o_send.at[b, peer], recv_sem=o_recv.at[b, p],
            device_id=at_member(zh * half + peer), device_id_type=MESH,
        )

    def o_arrival(b, d):
        peer = p ^ d
        return pltpu.make_async_remote_copy(
            src_ref=upd.at[b, pl.ds(peer * mem_local, mem_local)],
            dst_ref=out_hbm.at[
                :, pl.ds(pl.multiple_of(peer * chunk_rows, chunk_rows), chunk_rows), pl.ds(b * LANE, LANE)
            ],
            send_sem=o_send.at[b, peer], recv_sem=o_recv.at[b, peer],
            device_id=at_member(zh * half + peer), device_id_type=MESH,
        )

    flat = th_all.reshape(blocks * members * chunk_rows, LANE)
    upd_flat = upd.reshape(blocks * half_members * chunk_rows, LANE)
    own_out = []
    for b in range(blocks):
        at_b = b * members * chunk_rows
        lax.fori_loop(b * half, (b + 1) * half, wait_recv(far_arrival), 0)
        for r in range(0, chunk_rows, 2):
            field = jnp.concatenate(
                [flat[pl.ds(at_b + r + k, members, stride=chunk_rows), :] for k in range(2)], axis=1
            )
            hi = field.astype(BF16)
            lo_part = (field - hi.astype(F32)).astype(BF16)
            both = jnp.dot(lhs, jnp.concatenate([hi, lo_part], axis=0), preferred_element_type=F32)
            both = both[:half_members] + both[half_members:]
            for k in range(2):
                own = flat[pl.ds(at_b + zh * (half_members * chunk_rows) + r + k, half_members, stride=chunk_rows), :]
                upd_flat[pl.ds(b * half_members * chunk_rows + r + k, half_members, stride=chunk_rows), :] = (
                    own + both[:, k * LANE : (k + 1) * LANE]
                )
        lax.fori_loop(1, half, start(functools.partial(o_copy, b)), 0)
        own_out.append(
            pltpu.make_async_copy(
                upd.at[b, pl.ds(p * mem_local, mem_local)],
                out_hbm.at[:, pl.ds(own_chunk, chunk_rows), pl.ds(b * LANE, LANE)],
                in_sem.at[4 + b],
            )
        )
        own_out[b].start()

    for copy in halos:
        copy.wait_send()
    lax.fori_loop(1, half, wait_send(e_copy), 0)
    lax.fori_loop(1, half, wait_send(th_copy), 0)
    lax.fori_loop(0, blocks * half, wait_send(far_copy), 0)
    lax.fori_loop(1, half + 1, wait_send(p_copy), 0)
    lax.fori_loop(1, half, wait_send(p_relay), 0)
    lax.fori_loop(1, tiles, wait_send(r_copy), 0)
    lax.fori_loop(1, half, wait_send(a_copy), 0)
    for b in range(blocks):
        own_out[b].wait()
        lax.fori_loop(1, half, wait_recv(functools.partial(o_arrival, b)), 0)
        lax.fori_loop(1, half, wait_send(functools.partial(o_copy, b)), 0)


def on_device(sizes, theta, tracer, velocity, obs_index, observed, noise_var, obs_perturb):
    n_mem, n_lat, n_lon = sizes
    mem_local, rows, cols = theta.shape
    obs = obs_index.shape[0]
    half = n_mem // 2
    tiles = n_lat * n_lon
    members = n_mem * mem_local
    half_members = members // 2
    chunk_rows = rows // half
    planes = mem_local + 6
    pad_rows, pad_cols = rows + 2 * SUB, cols + LANE
    g_rows = half * SUB * -(-(members + half_members) // (half * SUB))
    folded = [a.reshape(obs // LANE, LANE) for a in (obs_index, observed, noise_var)]
    dma = pltpu.SemaphoreType.DMA
    theta_new, pred = pl.pallas_call(
        functools.partial(kernel, sizes),
        out_shape=(
            jax.ShapeDtypeStruct(theta.shape, F32),
            jax.ShapeDtypeStruct((mem_local, obs), F32),
        ),
        in_specs=[
            pl.BlockSpec(memory_space=pl.ANY),
            pl.BlockSpec(memory_space=pl.ANY),
            pl.BlockSpec(memory_space=pl.ANY),
            pl.BlockSpec(memory_space=pltpu.SMEM),
            pl.BlockSpec(memory_space=pltpu.VMEM),
            pl.BlockSpec(memory_space=pltpu.VMEM),
            pl.BlockSpec(memory_space=pltpu.VMEM),
            pl.BlockSpec(memory_space=pltpu.VMEM),
        ],
        out_specs=(pl.BlockSpec(memory_space=pl.ANY), pl.BlockSpec(memory_space=pltpu.VMEM)),
        scratch_shapes=[
            pltpu.VMEM((cols // LANE, mem_local, rows, LANE), F32),
            pltpu.VMEM((planes, pad_rows, pad_cols), F32),
            pltpu.VMEM((planes, SUB, cols), F32),
            pltpu.VMEM((rows, LANE), F32),
            pltpu.VMEM((rows, LANE), F32),
            pltpu.VMEM((pad_rows, LANE), F32),
            pltpu.VMEM((pad_rows, LANE), F32),
            pltpu.VMEM((2, pad_rows, pad_cols), F32),
            pltpu.VMEM((2, 4, pad_rows, pad_cols), F32),
            pltpu.VMEM((mem_local, 4, pad_rows, pad_cols), F32),
            pltpu.VMEM((mem_local, 2, pad_rows, pad_cols), F32),
            pltpu.VMEM((rows * (cols // LANE), SUB, LANE), F32),
            pltpu.VMEM((cols // LANE, members, chunk_rows, LANE), F32),
            pltpu.VMEM((half, SUB, obs // 2), F32),
            pltpu.VMEM((n_mem, SUB, obs // 2), F32),
            pltpu.VMEM((members, obs), F32),
            pltpu.VMEM((members, obs), F32),
            pltpu.VMEM((members + half_members, obs), F32),
            pltpu.VMEM((g_rows, members), F32),
            pltpu.VMEM((tiles, g_rows // half, members), F32),
            pltpu.VMEM((g_rows, members), F32),
            pltpu.VMEM((members, members), F32),
            pltpu.VMEM((cols // LANE, half_members, chunk_rows, LANE), F32),
            dma((4 + cols // LANE,)),
            dma((5,)), dma((5,)),
            dma((n_mem,)), dma((n_mem,)),
            dma((cols // LANE * half,)), dma((cols // LANE * half,)),
            dma((half,)), dma((half,)),
            dma((n_mem,)), dma((n_mem,)),
            dma((tiles,)), dma((tiles,)),
            dma((half,)), dma((half,)),
            dma((cols // LANE, half)), dma((cols // LANE, half)),
        ],
        compiler_params=pltpu.CompilerParams(
            collective_id=0, has_side_effects=True, vmem_limit_bytes=56 * 1024 * 1024
        ),
        name="inversion",
    )(theta, tracer, velocity.reshape(4, rows, cols), obs_index, *folded, obs_perturb.T)
    return theta_new, pred.T


def solution(mesh):
    placed = (
        P("member", "lat", "lon"),
        P(None, "lat", "lon"),
        P(None, None, "lat", "lon"),
        P(("lat", "lon")),
        P(("lat", "lon")),
        P(("lat", "lon")),
        P(("lat", "lon"), "member"),
    )
    sizes = (mesh.shape["member"], mesh.shape["lat"], mesh.shape["lon"])
    return jax.shard_map(
        functools.partial(on_device, sizes),
        mesh=mesh,
        in_specs=placed,
        out_specs=(P("member", "lat", "lon"), P(("lat", "lon"), "member")),
        check_vma=False,
    )
```

```python
import functools

import jax
import jax.numpy as jnp
from jax import lax
from jax.experimental import pallas as pl
from jax.experimental.pallas import tpu as pltpu
from jax.sharding import PartitionSpec as P

LM = 1.0
MESH = pl.DeviceIdType.MESH
F32 = jnp.float32
BF16 = jnp.bfloat16
LANE = 128
SUB = 8
FAR = (6, 6, 6, 4, 0, 8, 6, 6)


def lane_shift(x, by):
    return pltpu.roll(x, by % x.shape[1], axis=1)


def south_of(prev, cur):
    return jnp.concatenate([prev[SUB - 1 :], cur[: SUB - 1]], axis=0)


def north_of(cur, nxt):
    return jnp.concatenate([cur[1:], nxt[:1]], axis=0)


def invert(mat):
    n = mat.shape[0]
    shape = (SUB, n)
    row_id = lax.broadcasted_iota(jnp.int32, shape, 0)
    lane_id = lax.broadcasted_iota(jnp.int32, shape, 1)

    def row(x, r):
        return jnp.broadcast_to(x[r : r + 1, :], shape)

    row_all = lax.broadcasted_iota(jnp.int32, (n, n), 0)
    lane_all = lax.broadcasted_iota(jnp.int32, (n, n), 1)

    def spread(old, first, panel):
        wide = jnp.concatenate([panel] * (n // SUB), axis=0)
        wide = jnp.where((row_all >= first) & (row_all < first + SUB), wide, 0.0)
        return jnp.dot(old, wide, precision=lax.Precision.HIGHEST, preferred_element_type=F32)

    def behind(first, panel):
        lanes = [jnp.full(shape, (first + c) & (n - 1), jnp.int32) for c in range(SUB)]
        rows = [row(panel, c) for c in range(SUB)]
        in_panel = (lane_id >= first) & (lane_id < first + SUB)

        def update(tile):
            parts = [
                jnp.take_along_axis(tile, lanes[c], axis=1, mode="promise_in_bounds") * rows[c] for c in range(SUB)
            ]
            while len(parts) > 1:
                parts = [parts[k] + parts[k + 1] for k in range(0, len(parts), 2)]
            return jnp.where(in_panel, 0.0, tile) - parts[0]

        return update

    def eliminate_panel(b, last):
        first = pl.multiple_of(b * SUB, SUB)
        update = behind(first - SUB, last)
        panel = update(mat[pl.ds(first, SUB), :])
        cols = [
            jnp.take_along_axis(panel, jnp.full(shape, first + c, jnp.int32), axis=1, mode="promise_in_bounds")
            for c in range(SUB)
        ]
        for c in range(0, SUB, 2):
            c0, c1 = cols[c], cols[c + 1]
            p00, p01, p11 = row(c0, c), row(c1, c), row(c1, c + 1)
            inv = 1.0 / (p00 * p11 - p01 * p01)
            i00, i01, i11 = p11 * inv, -p01 * inv, p00 * inv

            def eliminate(r0, r1, rest):
                new0 = i00 * r0 + i01 * r1
                new1 = i01 * r0 + i11 * r1
                rest = rest - c0 * new0 - c1 * new1
                return jnp.where(row_id == c, new0, jnp.where(row_id == c + 1, new1, rest))

            at0, at1 = lane_id == first + c, lane_id == first + c + 1
            for k in range(c + 2, SUB):
                cols[k] = eliminate(row(cols[k], c), row(cols[k], c + 1), cols[k])
            panel = eliminate(
                jnp.where(at0, 1.0, jnp.where(at1, 0.0, row(panel, c))),
                jnp.where(at0, 0.0, jnp.where(at1, 1.0, row(panel, c + 1))),
                jnp.where(at0 | at1, 0.0, panel),
            )
        old = mat[...]
        kept = (row_all >= first - SUB) & (row_all < first)
        left = (lane_all >= first - SUB) & (lane_all < first)
        mat[...] = jnp.where(kept, old, jnp.where(left, 0.0, old) - spread(old, first - SUB, last))
        mat[pl.ds(first, SUB), :] = panel
        return panel

    last = lax.fori_loop(0, n // SUB, eliminate_panel, jnp.zeros(shape, F32))
    old = mat[...]
    done = jnp.where(lane_all >= n - SUB, 0.0, old) - spread(old, n - SUB, last)
    mat[...] = jnp.where(row_all >= n - SUB, old, done)


def kernel(
    sizes,
    theta_hbm, tracer_hbm, velocity_hbm, obs_index, obs_cell_hbm, observed_hbm, noise_hbm, perturb_hbm,
    out_hbm, pred_out,
    obs_cell, observed_in, noise_in, perturb, th_own, x, lat_in, east_out, west_out, east_in, west_in,
    base, diffs, faces, c1, cells,
    th_all, e_all, pred_all, pred_mat, weighted, left, g_own, rs_in, ab, mat, upd,
    in_sem, small_sem, halo_send, halo_recv, th_send, th_recv, f_send, f_recv, e_send, e_recv, p_send, p_recv,
    r_send, r_recv, a_send, a_recv, o_send, o_recv,
):
    n_mem, n_lat, n_lon = sizes
    half = n_mem // 2
    tiles = n_lat * n_lon
    blocks, mem_local, rows, _ = th_own.shape
    planes, pad_rows, pad_cols = x.shape
    cols = blocks * LANE
    members = n_mem * mem_local
    half_members = members // 2
    chunk_rows = rows // half
    n_chunks = pad_rows // SUB
    obs = perturb.shape[1]
    obs_half = obs // 2
    g_rows = g_own.shape[0]
    part = g_rows // half
    scale = 1.0 / float(members - 1) ** 0.5

    m = lax.axis_index("member")
    la = lax.axis_index("lat")
    lo = lax.axis_index("lon")
    zh = lax.shift_right_logical(m, half.bit_length() - 1)
    p = m & (half - 1)
    t = la * n_lon + lo

    def at_member(peer):
        return {"member": peer, "lat": la, "lon": lo}

    def at_tile(peer):
        return {"member": m, "lat": lax.shift_right_logical(peer, n_lon.bit_length() - 1), "lon": peer & (n_lon - 1)}

    barrier = pltpu.get_barrier_semaphore()

    def greet_member(d, _):
        pl.semaphore_signal(barrier, inc=1, device_id=at_member(m ^ d), device_id_type=MESH)
        return 0

    def greet_tile(d, _):
        pl.semaphore_signal(barrier, inc=1, device_id=at_tile(t ^ d), device_id_type=MESH)
        return 0

    lax.fori_loop(1, n_mem, greet_member, 0)
    lax.fori_loop(1, tiles, greet_tile, 0)

    loads = [
        pltpu.make_async_copy(theta_hbm.at[:, :, pl.ds(b * LANE, LANE)], th_own.at[b], in_sem.at[4 + b])
        for b in range(blocks)
    ] + [
        pltpu.make_async_copy(
            tracer_hbm, x.at[pl.ds(mem_local, 2), pl.ds(SUB, rows), pl.ds(0, cols)], in_sem.at[1]
        ),
        pltpu.make_async_copy(
            velocity_hbm, x.at[pl.ds(mem_local + 2, 4), pl.ds(SUB, rows), pl.ds(0, cols)], in_sem.at[2]
        ),
    ]
    smalls = [
        pltpu.make_async_copy(src, dst, small_sem.at[i])
        for i, (src, dst) in enumerate(
            ((obs_cell_hbm, obs_cell), (observed_hbm, observed_in), (noise_hbm, noise_in), (perturb_hbm, perturb))
        )
    ]
    for load in loads + smalls:
        load.start()

    for load in loads[:blocks]:
        load.wait()

    def make_kappa(i, _):
        r = pl.multiple_of(i * SUB, SUB)
        for j in range(mem_local):
            for b in range(blocks):
                x[j, pl.ds(r + SUB, SUB), pl.ds(b * LANE, LANE)] = 0.1 * jax.nn.sigmoid(
                    th_own[b, j, pl.ds(r, SUB), :]
                )
        return 0

    lax.fori_loop(0, rows // SUB, make_kappa, 0)
    for load in loads[blocks:]:
        load.wait()

    lane8 = lax.broadcasted_iota(jnp.int32, (SUB, LANE), 1)
    sub8 = lax.broadcasted_iota(jnp.int32, (SUB, LANE), 0)

    def pack(i, _):
        r = pl.multiple_of(i * SUB, SUB)
        east = jnp.zeros((SUB, LANE), F32)
        west = jnp.zeros((SUB, LANE), F32)
        for q in range(planes):
            first = x[q, pl.ds(r + SUB, SUB), pl.ds(0, LANE)]
            last = x[q, pl.ds(r + SUB, SUB), pl.ds(cols - LANE, LANE)]
            east = jnp.where((lane8 // 2) == q, lane_shift(first, 2 * q), east)
            west = jnp.where(((LANE - 1 - lane8) // 2) == q, lane_shift(last, -2 * q), west)
        east_out[pl.ds(r, SUB), :] = east
        west_out[pl.ds(r, SUB), :] = west
        return 0

    lax.fori_loop(0, rows // SUB, pack, 0)

    pl.semaphore_wait(barrier, n_mem - 1 + tiles - 1)

    my_edge = pl.multiple_of((1 - la) * (rows - SUB), SUB)
    their_edge = pl.multiple_of(la * (rows + SUB), SUB)
    lo_w = (lo + n_lon - 1) & (n_lon - 1)
    lo_e = (lo + 1) & (n_lon - 1)

    def halo(i, src, dst, lat, lon):
        return pltpu.make_async_remote_copy(
            src_ref=src, dst_ref=dst, send_sem=halo_send.at[i], recv_sem=halo_recv.at[i],
            device_id={"member": m, "lat": lat, "lon": lon}, device_id_type=MESH,
        )

    halos = [
        halo(0, east_out, east_in.at[pl.ds(SUB, rows), :], la, lo_w),
        halo(1, west_out, west_in.at[pl.ds(SUB, rows), :], la, lo_e),
        halo(2, east_out.at[pl.ds(my_edge, SUB), :], east_in.at[pl.ds(their_edge, SUB), :], 1 - la, lo_w),
        halo(3, west_out.at[pl.ds(my_edge, SUB), :], west_in.at[pl.ds(their_edge, SUB), :], 1 - la, lo_e),
        halo(4, x.at[:, pl.ds(my_edge + SUB, SUB), pl.ds(0, cols)], lat_in, 1 - la, lo),
    ]
    for copy in halos:
        copy.start()

    far = [0]

    def send_far(count):
        lax.fori_loop(far[0], far[0] + count, start(far_copy), 0)
        far[0] += count

    def e_copy(d):
        peer = p ^ d
        return pltpu.make_async_remote_copy(
            src_ref=e_all.at[p], dst_ref=e_all.at[p], send_sem=e_send.at[peer], recv_sem=e_recv.at[p],
            device_id=at_member(zh * half + peer), device_id_type=MESH,
        )

    def e_arrival(d):
        peer = p ^ d
        return pltpu.make_async_remote_copy(
            src_ref=e_all.at[p], dst_ref=e_all.at[peer], send_sem=e_send.at[peer], recv_sem=e_recv.at[peer],
            device_id=at_member(zh * half + peer), device_id_type=MESH,
        )

    def th_copy(d):
        peer = m ^ d
        r = pl.multiple_of((peer & (half - 1)) * chunk_rows, chunk_rows)
        return pltpu.make_async_remote_copy(
            src_ref=th_own.at[:, :, pl.ds(r, chunk_rows), :],
            dst_ref=th_all.at[:, pl.ds(m * mem_local, mem_local)],
            send_sem=th_send.at[peer], recv_sem=th_recv.at[m],
            device_id=at_member(peer), device_id_type=MESH,
        )

    def th_arrival(d):
        peer = m ^ d
        return pltpu.make_async_remote_copy(
            src_ref=th_own.at[:, :, pl.ds(0, chunk_rows), :],
            dst_ref=th_all.at[:, pl.ds(peer * mem_local, mem_local)],
            send_sem=th_send.at[peer], recv_sem=th_recv.at[peer],
            device_id=at_member(peer), device_id_type=MESH,
        )

    def far_copy(i):
        b, d = i // half, half + (i & (half - 1))
        peer = m ^ d
        r = pl.multiple_of((peer & (half - 1)) * chunk_rows, chunk_rows)
        return pltpu.make_async_remote_copy(
            src_ref=th_own.at[b, :, pl.ds(r, chunk_rows), :],
            dst_ref=th_all.at[b, pl.ds(m * mem_local, mem_local)],
            send_sem=f_send.at[i], recv_sem=f_recv.at[i],
            device_id=at_member(peer), device_id_type=MESH,
        )

    def far_arrival(i):
        b, d = i // half, half + (i & (half - 1))
        peer = m ^ d
        return pltpu.make_async_remote_copy(
            src_ref=th_own.at[b, :, pl.ds(0, chunk_rows), :],
            dst_ref=th_all.at[b, pl.ds(peer * mem_local, mem_local)],
            send_sem=f_send.at[i], recv_sem=f_recv.at[i],
            device_id=at_member(peer), device_id_type=MESH,
        )

    def start(copy):
        def body(d, _):
            copy(d).start()
            return 0
        return body

    def wait_recv(copy):
        def body(d, _):
            copy(d).wait_recv()
            return 0
        return body

    def wait_send(copy):
        def body(d, _):
            copy(d).wait_send()
            return 0
        return body

    lax.fori_loop(1, half, start(th_copy), 0)
    own_chunk = pl.multiple_of(p * chunk_rows, chunk_rows)
    own_th = pltpu.make_async_copy(
        th_own.at[:, :, pl.ds(own_chunk, chunk_rows), :],
        th_all.at[:, pl.ds(m * mem_local, mem_local)],
        in_sem.at[3],
    )
    own_th.start()
    send_far(FAR[0])

    for load in smalls:
        load.wait()

    def row_of(ref):
        return jnp.concatenate([ref[b : b + 1, :] for b in range(obs // LANE)], axis=1)

    observed = row_of(observed_in)
    noise = row_of(noise_in)
    inv_noise = 1.0 / noise
    e_own = observed + jnp.sqrt(noise) * perturb[...]
    e_all[p, 0:mem_local, :] = e_own[:, :obs_half]
    e_all[p, mem_local:SUB, :] = e_own[:, obs_half:]

    for copy in halos:
        copy.wait_recv()
    lax.fori_loop(1, half, start(e_copy), 0)

    send_far(FAR[1])

    for q in range(planes):
        block = lat_in[q]
        x[q, 0:SUB, 0:cols] = jnp.where(la == 1, block, 0.0)
        x[q, pad_rows - SUB : pad_rows, 0:cols] = jnp.where(la == 0, block, 0.0)

    def unpack(i, _):
        r = pl.multiple_of(i * SUB, SUB)
        inside = ((i > 0) | (la == 1)) & ((i < n_chunks - 1) | (la == 0))
        east = jnp.where(inside, east_in[pl.ds(r, SUB), :], 0.0)
        west = jnp.where(inside, west_in[pl.ds(r, SUB), :], 0.0)
        for q in range(planes):
            x[q, pl.ds(r, SUB), pl.ds(cols, LANE)] = jnp.where(
                lane8 < LANE // 2, lane_shift(east, -2 * q), lane_shift(west, 2 * q)
            )
        return 0

    lax.fori_loop(0, n_chunks, unpack, 0)

    def shared(i, _):
        r = pl.multiple_of(i * SUB, SUB)
        before = pl.multiple_of(jnp.maximum(i - 1, 0) * SUB, SUB)
        after = pl.multiple_of(jnp.minimum(i + 1, n_chunks - 1) * SUB, SUB)
        cur = [x[mem_local + l, pl.ds(r, SUB), :] for l in range(2)]
        for l in range(2):
            c = cur[l]
            u = x[mem_local + 2 + l, pl.ds(r, SUB), :]
            v = x[mem_local + 4 + l, pl.ds(r, SUB), :]
            d_w = lane_shift(c, 1) - c
            d_e = lane_shift(c, -1) - c
            d_s = south_of(x[mem_local + l, pl.ds(before, SUB), :], c) - c
            d_n = north_of(c, x[mem_local + l, pl.ds(after, SUB), :]) - c
            adv = jnp.maximum(u, 0.0) * d_w - jnp.minimum(u, 0.0) * d_e
            adv = adv + jnp.maximum(v, 0.0) * d_s - jnp.minimum(v, 0.0) * d_n
            base[l, pl.ds(r, SUB), :] = c + adv + 0.2 * (cur[1 - l] - c)
            for k, d in enumerate((d_w, d_e, d_s, d_n)):
                diffs[l, k, pl.ds(r, SUB), :] = d
        return 0

    lax.fori_loop(0, n_chunks, shared, 0)
    send_far(FAR[2])

    def first_step(i, _):
        r = pl.multiple_of(i * SUB, SUB)
        before = pl.multiple_of(jnp.maximum(i - 1, 0) * SUB, SUB)
        after = pl.multiple_of(jnp.minimum(i + 1, n_chunks - 1) * SUB, SUB)
        inside = ((i > 0) | (la == 1)) & ((i < n_chunks - 1) | (la == 0))
        for j in range(mem_local):
            k = x[j, pl.ds(r, SUB), :]
            f_e = 0.5 * (k + lane_shift(k, -1))
            f_w = lane_shift(f_e, 1)
            f_s = 0.5 * (k + south_of(x[j, pl.ds(before, SUB), :], k))
            f_n = 0.5 * (k + north_of(k, x[j, pl.ds(after, SUB), :]))
            for n, f in enumerate((f_w, f_e, f_s, f_n)):
                faces[j, n, pl.ds(r, SUB), :] = f
            for l in range(2):
                c = base[l, pl.ds(r, SUB), :]
                for n, f in enumerate((f_w, f_e, f_s, f_n)):
                    c = c + f * diffs[l, n, pl.ds(r, SUB), :]
                c1[j, l, pl.ds(r, SUB), :] = jnp.where(inside, c, 0.0)
        return 0

    lax.fori_loop(0, n_chunks, first_step, 0)
    send_far(FAR[3])

    flat_cells = cells.reshape(rows * blocks * SUB, LANE)

    def second_step(i, _):
        r = pl.multiple_of(i * SUB, SUB)
        before = pl.multiple_of((i - 1) * SUB, SUB)
        after = pl.multiple_of((i + 1) * SUB, SUB)
        u = x[mem_local + 2, pl.ds(r, SUB), pl.ds(0, cols)]
        v = x[mem_local + 4, pl.ds(r, SUB), pl.ds(0, cols)]
        winds = (jnp.maximum(u, 0.0), -jnp.minimum(u, 0.0), jnp.maximum(v, 0.0), -jnp.minimum(v, 0.0))
        for j in range(mem_local):
            wide = c1[j, 0, pl.ds(r, SUB), :]
            c = wide[:, :cols]
            sides = (
                lane_shift(wide, 1)[:, :cols],
                lane_shift(wide, -1)[:, :cols],
                south_of(c1[j, 0, pl.ds(before, SUB), pl.ds(0, cols)], c),
                north_of(c, c1[j, 0, pl.ds(after, SUB), pl.ds(0, cols)]),
            )
            new = c + 0.2 * (c1[j, 1, pl.ds(r, SUB), pl.ds(0, cols)] - c)
            for n in range(4):
                new = new + (winds[n] + faces[j, n, pl.ds(r, SUB), pl.ds(0, cols)]) * (sides[n] - c)
            for b in range(blocks):
                first = ((i - 1) * SUB * blocks + b) * SUB + j
                piece = new[:, b * LANE : (b + 1) * LANE]
                flat_cells[pl.ds(first, SUB, stride=SUB * blocks), :] = piece
                flat_cells[pl.ds(first + mem_local, SUB, stride=SUB * blocks), :] = piece
        return 0

    lax.fori_loop(1, n_chunks - 1, second_step, 0)
    send_far(FAR[4])

    obs_blocks = obs // LANE
    step_of = 8
    low8 = sub8 < mem_local
    obs_lane = [
        jnp.where(
            low8,
            jnp.broadcast_to(obs_cell[a : a + 1, :], (SUB, LANE)),
            jnp.broadcast_to(obs_cell[a + obs_blocks // 2 : a + obs_blocks // 2 + 1, :], (SUB, LANE)),
        )
        & (LANE - 1)
        for a in range(obs_blocks // 2)
    ]

    def gather(i, accs):
        accs = list(accs)
        for k in range(step_of):
            s = i * step_of + k
            here = lane8 == s
            for a in range(obs_blocks // 2):
                got = [
                    cells[lax.shift_right_logical(obs_index[b * LANE + s], LANE.bit_length() - 1)]
                    for b in (a, a + obs_blocks // 2)
                ]
                got = jnp.where(low8, got[0], got[1])
                got = jnp.take_along_axis(got, obs_lane[a], axis=1, mode="promise_in_bounds")
                accs[a] = jnp.where(here, got, accs[a])
        return tuple(accs)

    accs = lax.fori_loop(
        0, LANE // step_of, gather, tuple(jnp.zeros((SUB, LANE), F32) for _ in range(obs_blocks // 2))
    )
    own_pred = jnp.concatenate(accs, axis=1)
    pred_all[m] = own_pred
    pred_out[:, 0:obs_half] = own_pred[0:mem_local]
    pred_out[:, obs_half:obs] = own_pred[mem_local:SUB]

    def p_copy(d):
        peer = m ^ d
        return pltpu.make_async_remote_copy(
            src_ref=pred_all.at[m], dst_ref=pred_all.at[m], send_sem=p_send.at[peer], recv_sem=p_recv.at[m],
            device_id=at_member(peer), device_id_type=MESH,
        )

    def p_arrival(d):
        peer = m ^ d
        return pltpu.make_async_remote_copy(
            src_ref=pred_all.at[m], dst_ref=pred_all.at[peer], send_sem=p_send.at[peer], recv_sem=p_recv.at[peer],
            device_id=at_member(peer), device_id_type=MESH,
        )

    def p_relay(d):
        far_slot = m ^ half
        return pltpu.make_async_remote_copy(
            src_ref=pred_all.at[far_slot], dst_ref=pred_all.at[far_slot],
            send_sem=p_send.at[far_slot ^ d], recv_sem=p_recv.at[far_slot],
            device_id=at_member(m ^ d), device_id_type=MESH,
        )

    p_copy(half).start()
    lax.fori_loop(1, half, start(p_copy), 0)
    send_far(FAR[5])
    lax.fori_loop(1, half, wait_recv(e_arrival), 0)
    p_arrival(half).wait_recv()
    lax.fori_loop(1, half, start(p_relay), 0)
    lax.fori_loop(1, half, wait_recv(p_arrival), 0)
    lax.fori_loop(half + 1, n_mem, wait_recv(p_arrival), 0)

    low = lax.broadcasted_iota(jnp.int32, (SUB, obs_half), 0) < mem_local

    def unfold(a, b):
        top = jnp.where(low, a, pltpu.roll(b, mem_local, axis=0))
        bottom = jnp.where(low, pltpu.roll(a, mem_local, axis=0), b)
        return jnp.concatenate([top, bottom], axis=1)

    def collect(i, total):
        both = unfold(pred_all[2 * i], pred_all[2 * i + 1])
        pred_mat[pl.ds(pl.multiple_of(i * SUB, SUB), SUB), :] = both
        return total + both

    total = lax.fori_loop(0, n_mem // 2, collect, jnp.zeros((SUB, obs), F32))
    mean = jnp.sum(total, axis=0, keepdims=True) * (1.0 / members)

    def center(i, _):
        r = pl.multiple_of(i * SUB, SUB)
        anom = (pred_mat[pl.ds(r, SUB), :] - mean) * scale
        left[pl.ds(r, SUB), :] = anom
        weighted[pl.ds(r, SUB), :] = anom * inv_noise
        return 0

    lax.fori_loop(0, members // SUB, center, 0)

    def innovate(i, _):
        r = pl.multiple_of(zh * half_members + i * SUB, SUB)
        e = unfold(e_all[2 * i], e_all[2 * i + 1])
        left[pl.ds(pl.multiple_of(members + i * SUB, SUB), SUB), :] = e - pred_mat[pl.ds(r, SUB), :]
        return 0

    lax.fori_loop(0, half_members // SUB, innovate, 0)

    g_own[members + half_members :, :] = jnp.zeros((g_rows - members - half_members, members), F32)
    g_own[0 : members + half_members, :] = lax.dot_general(
        left[...], weighted[...], (((1,), (1,)), ((), ())), precision=lax.Precision.HIGHEST,
        preferred_element_type=F32,
    )

    my_part = pl.multiple_of(p * part, SUB)

    def r_copy(d):
        peer = t ^ d
        return pltpu.make_async_remote_copy(
            src_ref=g_own.at[pl.ds(my_part, part), :], dst_ref=rs_in.at[t],
            send_sem=r_send.at[peer], recv_sem=r_recv.at[t],
            device_id=at_tile(peer), device_id_type=MESH,
        )

    def r_arrival(d):
        peer = t ^ d
        return pltpu.make_async_remote_copy(
            src_ref=g_own.at[pl.ds(0, part), :], dst_ref=rs_in.at[peer],
            send_sem=r_send.at[peer], recv_sem=r_recv.at[peer],
            device_id=at_tile(peer), device_id_type=MESH,
        )

    lax.fori_loop(1, tiles, start(r_copy), 0)
    send_far(FAR[6])
    rs_in[t] = g_own[pl.ds(my_part, part), :]
    lax.fori_loop(1, tiles, wait_recv(r_arrival), 0)
    total_part = rs_in[0]
    for k in range(1, tiles):
        total_part = total_part + rs_in[k]
    ab[pl.ds(my_part, part), :] = total_part

    def a_copy(d):
        peer = p ^ d
        mine = ab.at[pl.ds(my_part, part), :]
        return pltpu.make_async_remote_copy(
            src_ref=mine, dst_ref=mine, send_sem=a_send.at[peer], recv_sem=a_recv.at[p],
            device_id=at_member(zh * half + peer), device_id_type=MESH,
        )

    def a_arrival(d):
        peer = p ^ d
        return pltpu.make_async_remote_copy(
            src_ref=ab.at[pl.ds(my_part, part), :],
            dst_ref=ab.at[pl.ds(pl.multiple_of(peer * part, SUB), part), :],
            send_sem=a_send.at[peer], recv_sem=a_recv.at[peer],
            device_id=at_member(zh * half + peer), device_id_type=MESH,
        )

    lax.fori_loop(1, half, start(a_copy), 0)
    send_far(FAR[7])
    lax.fori_loop(1, half, wait_recv(a_arrival), 0)

    send_far(blocks * half - far[0])
    eye = lax.broadcasted_iota(jnp.int32, (members, members), 0) == lax.broadcasted_iota(
        jnp.int32, (members, members), 1
    )
    mat[...] = ab[0:members, :] + jnp.where(eye, LM, 0.0)
    invert(mat)
    w = jnp.dot(
        ab[members : members + half_members, :], mat[...], precision=lax.Precision.HIGHEST,
        preferred_element_type=F32,
    )
    w = scale * (w - jnp.mean(w, axis=1, keepdims=True))
    w_hi = w.astype(BF16)
    w_lo = (w - w_hi.astype(F32)).astype(BF16)
    lhs = jnp.concatenate(
        [jnp.concatenate([w_hi, w_hi], axis=1), jnp.concatenate([w_lo, jnp.zeros_like(w_lo)], axis=1)], axis=0
    )

    own_th.wait()
    lax.fori_loop(1, half, wait_recv(th_arrival), 0)


    def o_copy(b, d):
        peer = p ^ d
        return pltpu.make_async_remote_copy(
            src_ref=upd.at[b, pl.ds(peer * mem_local, mem_local)],
            dst_ref=out_hbm.at[:, pl.ds(own_chunk, chunk_rows), pl.ds(b * LANE, LANE)],
            send_sem=o_send.at[b, peer], recv_sem=o_recv.at[b, p],
            device_id=at_member(zh * half + peer), device_id_type=MESH,
        )

    def o_arrival(b, d):
        peer = p ^ d
        return pltpu.make_async_remote_copy(
            src_ref=upd.at[b, pl.ds(peer * mem_local, mem_local)],
            dst_ref=out_hbm.at[
                :, pl.ds(pl.multiple_of(peer * chunk_rows, chunk_rows), chunk_rows), pl.ds(b * LANE, LANE)
            ],
            send_sem=o_send.at[b, peer], recv_sem=o_recv.at[b, peer],
            device_id=at_member(zh * half + peer), device_id_type=MESH,
        )

    flat = th_all.reshape(blocks * members * chunk_rows, LANE)
    upd_flat = upd.reshape(blocks * half_members * chunk_rows, LANE)
    own_out = []
    for b in range(blocks):
        at_b = b * members * chunk_rows
        lax.fori_loop(b * half, (b + 1) * half, wait_recv(far_arrival), 0)
        for r in range(0, chunk_rows, 2):
            field = jnp.concatenate(
                [flat[pl.ds(at_b + r + k, members, stride=chunk_rows), :] for k in range(2)], axis=1
            )
            hi = field.astype(BF16)
            lo_part = (field - hi.astype(F32)).astype(BF16)
            both = jnp.dot(lhs, jnp.concatenate([hi, lo_part], axis=0), preferred_element_type=F32)
            both = both[:half_members] + both[half_members:]
            for k in range(2):
                own = flat[pl.ds(at_b + zh * (half_members * chunk_rows) + r + k, half_members, stride=chunk_rows), :]
                upd_flat[pl.ds(b * half_members * chunk_rows + r + k, half_members, stride=chunk_rows), :] = (
                    own + both[:, k * LANE : (k + 1) * LANE]
                )
        lax.fori_loop(1, half, start(functools.partial(o_copy, b)), 0)
        own_out.append(
            pltpu.make_async_copy(
                upd.at[b, pl.ds(p * mem_local, mem_local)],
                out_hbm.at[:, pl.ds(own_chunk, chunk_rows), pl.ds(b * LANE, LANE)],
                in_sem.at[4 + b],
            )
        )
        own_out[b].start()

    for copy in halos:
        copy.wait_send()
    lax.fori_loop(1, half, wait_send(e_copy), 0)
    lax.fori_loop(1, half, wait_send(th_copy), 0)
    lax.fori_loop(0, blocks * half, wait_send(far_copy), 0)
    lax.fori_loop(1, half + 1, wait_send(p_copy), 0)
    lax.fori_loop(1, half, wait_send(p_relay), 0)
    lax.fori_loop(1, tiles, wait_send(r_copy), 0)
    lax.fori_loop(1, half, wait_send(a_copy), 0)
    for b in range(blocks):
        own_out[b].wait()
        lax.fori_loop(1, half, wait_recv(functools.partial(o_arrival, b)), 0)
        lax.fori_loop(1, half, wait_send(functools.partial(o_copy, b)), 0)


def on_device(sizes, theta, tracer, velocity, obs_index, observed, noise_var, obs_perturb):
    n_mem, n_lat, n_lon = sizes
    mem_local, rows, cols = theta.shape
    obs = obs_index.shape[0]
    half = n_mem // 2
    tiles = n_lat * n_lon
    members = n_mem * mem_local
    half_members = members // 2
    chunk_rows = rows // half
    planes = mem_local + 6
    pad_rows, pad_cols = rows + 2 * SUB, cols + LANE
    g_rows = half * SUB * -(-(members + half_members) // (half * SUB))
    folded = [a.reshape(obs // LANE, LANE) for a in (obs_index, observed, noise_var)]
    dma = pltpu.SemaphoreType.DMA
    theta_new, pred = pl.pallas_call(
        functools.partial(kernel, sizes),
        out_shape=(
            pltpu.VMEM(theta.shape, F32),
            pltpu.VMEM((mem_local, obs), F32),
        ),
        in_specs=[
            pl.BlockSpec(memory_space=pl.ANY),
            pl.BlockSpec(memory_space=pl.ANY),
            pl.BlockSpec(memory_space=pl.ANY),
            pl.BlockSpec(memory_space=pltpu.SMEM),
            pl.BlockSpec(memory_space=pl.ANY),
            pl.BlockSpec(memory_space=pl.ANY),
            pl.BlockSpec(memory_space=pl.ANY),
            pl.BlockSpec(memory_space=pl.ANY),
        ],
        out_specs=(pl.BlockSpec(memory_space=pl.ANY), pl.BlockSpec(memory_space=pltpu.VMEM)),
        scratch_shapes=[
            pltpu.VMEM((obs // LANE, LANE), jnp.int32),
            pltpu.VMEM((obs // LANE, LANE), F32),
            pltpu.VMEM((obs // LANE, LANE), F32),
            pltpu.VMEM((mem_local, obs), F32),
            pltpu.VMEM((cols // LANE, mem_local, rows, LANE), F32),
            pltpu.VMEM((planes, pad_rows, pad_cols), F32),
            pltpu.VMEM((planes, SUB, cols), F32),
            pltpu.VMEM((rows, LANE), F32),
            pltpu.VMEM((rows, LANE), F32),
            pltpu.VMEM((pad_rows, LANE), F32),
            pltpu.VMEM((pad_rows, LANE), F32),
            pltpu.VMEM((2, pad_rows, pad_cols), F32),
            pltpu.VMEM((2, 4, pad_rows, pad_cols), F32),
            pltpu.VMEM((mem_local, 4, pad_rows, pad_cols), F32),
            pltpu.VMEM((mem_local, 2, pad_rows, pad_cols), F32),
            pltpu.VMEM((rows * (cols // LANE), SUB, LANE), F32),
            pltpu.VMEM((cols // LANE, members, chunk_rows, LANE), F32),
            pltpu.VMEM((half, SUB, obs // 2), F32),
            pltpu.VMEM((n_mem, SUB, obs // 2), F32),
            pltpu.VMEM((members, obs), F32),
            pltpu.VMEM((members, obs), F32),
            pltpu.VMEM((members + half_members, obs), F32),
            pltpu.VMEM((g_rows, members), F32),
            pltpu.VMEM((tiles, g_rows // half, members), F32),
            pltpu.VMEM((g_rows, members), F32),
            pltpu.VMEM((members, members), F32),
            pltpu.VMEM((cols // LANE, half_members, chunk_rows, LANE), F32),
            dma((4 + cols // LANE,)),
            dma((4,)),
            dma((5,)), dma((5,)),
            dma((n_mem,)), dma((n_mem,)),
            dma((cols // LANE * half,)), dma((cols // LANE * half,)),
            dma((half,)), dma((half,)),
            dma((n_mem,)), dma((n_mem,)),
            dma((tiles,)), dma((tiles,)),
            dma((half,)), dma((half,)),
            dma((cols // LANE, half)), dma((cols // LANE, half)),
        ],
        compiler_params=pltpu.CompilerParams(
            collective_id=0, has_side_effects=True, vmem_limit_bytes=56 * 1024 * 1024
        ),
        name="inversion",
    )(theta, tracer, velocity.reshape(4, rows, cols), obs_index, *folded, obs_perturb.T)
    return theta_new, pred.T


def solution(mesh):
    placed = (
        P("member", "lat", "lon"),
        P(None, "lat", "lon"),
        P(None, None, "lat", "lon"),
        P(("lat", "lon")),
        P(("lat", "lon")),
        P(("lat", "lon")),
        P(("lat", "lon"), "member"),
    )
    sizes = (mesh.shape["member"], mesh.shape["lat"], mesh.shape["lon"])
    return jax.shard_map(
        functools.partial(on_device, sizes),
        mesh=mesh,
        in_specs=placed,
        out_specs=(P("member", "lat", "lon"), P(("lat", "lon"), "member")),
        check_vma=False,
    )
```

```python
import functools

import jax
import jax.numpy as jnp
from jax import lax
from jax.experimental import pallas as pl
from jax.experimental.pallas import tpu as pltpu
from jax.sharding import PartitionSpec as P

LM = 1.0
MESH = pl.DeviceIdType.MESH
F32 = jnp.float32
BF16 = jnp.bfloat16
LANE = 128
SUB = 8
FAR = (6, 6, 6, 4, 0, 8, 6, 6)


def lane_shift(x, by):
    return pltpu.roll(x, by % x.shape[1], axis=1)


def south_of(prev, cur):
    return jnp.concatenate([prev[SUB - 1 :], cur[: SUB - 1]], axis=0)


def north_of(cur, nxt):
    return jnp.concatenate([cur[1:], nxt[:1]], axis=0)


def invert(mat):
    n = mat.shape[0]
    shape = (SUB, n)
    row_id = lax.broadcasted_iota(jnp.int32, shape, 0)
    lane_id = lax.broadcasted_iota(jnp.int32, shape, 1)

    def row(x, r):
        return jnp.broadcast_to(x[r : r + 1, :], shape)

    row_all = lax.broadcasted_iota(jnp.int32, (n, n), 0)
    lane_all = lax.broadcasted_iota(jnp.int32, (n, n), 1)

    def spread(old, first, panel):
        wide = jnp.concatenate([panel] * (n // SUB), axis=0)
        wide = jnp.where((row_all >= first) & (row_all < first + SUB), wide, 0.0)
        return jnp.dot(old, wide, precision=lax.Precision.HIGHEST, preferred_element_type=F32)

    def behind(first, panel):
        lanes = [jnp.full(shape, (first + c) & (n - 1), jnp.int32) for c in range(SUB)]
        rows = [row(panel, c) for c in range(SUB)]
        in_panel = (lane_id >= first) & (lane_id < first + SUB)

        def update(tile):
            parts = [
                jnp.take_along_axis(tile, lanes[c], axis=1, mode="promise_in_bounds") * rows[c] for c in range(SUB)
            ]
            while len(parts) > 1:
                parts = [parts[k] + parts[k + 1] for k in range(0, len(parts), 2)]
            return jnp.where(in_panel, 0.0, tile) - parts[0]

        return update

    def eliminate_panel(b, last):
        first = pl.multiple_of(b * SUB, SUB)
        update = behind(first - SUB, last)
        panel = update(mat[pl.ds(first, SUB), :])
        cols = [
            jnp.take_along_axis(panel, jnp.full(shape, first + c, jnp.int32), axis=1, mode="promise_in_bounds")
            for c in range(SUB)
        ]
        for c in range(0, SUB, 2):
            c0, c1 = cols[c], cols[c + 1]
            p00, p01, p11 = row(c0, c), row(c1, c), row(c1, c + 1)
            inv = 1.0 / (p00 * p11 - p01 * p01)
            i00, i01, i11 = p11 * inv, -p01 * inv, p00 * inv

            def eliminate(r0, r1, rest):
                new0 = i00 * r0 + i01 * r1
                new1 = i01 * r0 + i11 * r1
                rest = rest - c0 * new0 - c1 * new1
                return jnp.where(row_id == c, new0, jnp.where(row_id == c + 1, new1, rest))

            at0, at1 = lane_id == first + c, lane_id == first + c + 1
            for k in range(c + 2, SUB):
                cols[k] = eliminate(row(cols[k], c), row(cols[k], c + 1), cols[k])
            panel = eliminate(
                jnp.where(at0, 1.0, jnp.where(at1, 0.0, row(panel, c))),
                jnp.where(at0, 0.0, jnp.where(at1, 1.0, row(panel, c + 1))),
                jnp.where(at0 | at1, 0.0, panel),
            )
        old = mat[...]
        kept = (row_all >= first - SUB) & (row_all < first)
        left = (lane_all >= first - SUB) & (lane_all < first)
        mat[...] = jnp.where(kept, old, jnp.where(left, 0.0, old) - spread(old, first - SUB, last))
        mat[pl.ds(first, SUB), :] = panel
        return panel

    last = lax.fori_loop(0, n // SUB, eliminate_panel, jnp.zeros(shape, F32))
    old = mat[...]
    done = jnp.where(lane_all >= n - SUB, 0.0, old) - spread(old, n - SUB, last)
    mat[...] = jnp.where(row_all >= n - SUB, old, done)


def kernel(
    sizes,
    theta_hbm, tracer_hbm, velocity_hbm, obs_index, obs_cell_hbm, observed_hbm, noise_hbm, perturb_hbm,
    out_hbm, pred_out,
    obs_cell, observed_in, noise_in, perturb, th_own, x, lat_in, east_out, west_out, east_in, west_in, east_rows, west_rows, east_got, west_got,
    base, diffs, faces, c1, cells,
    th_all, e_all, pred_all, pred_mat, weighted, left, g_own, rs_in, ab, mat, upd,
    in_sem, small_sem, halo_send, halo_recv, th_send, th_recv, f_send, f_recv, e_send, e_recv, p_send, p_recv,
    r_send, r_recv, a_send, a_recv, o_send, o_recv,
):
    n_mem, n_lat, n_lon = sizes
    half = n_mem // 2
    tiles = n_lat * n_lon
    blocks, mem_local, rows, _ = th_own.shape
    planes, pad_rows, pad_cols = x.shape
    cols = blocks * LANE
    members = n_mem * mem_local
    half_members = members // 2
    chunk_rows = rows // half
    n_chunks = pad_rows // SUB
    obs = perturb.shape[1]
    obs_half = obs // 2
    g_rows = g_own.shape[0]
    part = g_rows // half
    scale = 1.0 / float(members - 1) ** 0.5

    m = lax.axis_index("member")
    la = lax.axis_index("lat")
    lo = lax.axis_index("lon")
    zh = lax.shift_right_logical(m, half.bit_length() - 1)
    p = m & (half - 1)
    t = la * n_lon + lo

    def at_member(peer):
        return {"member": peer, "lat": la, "lon": lo}

    def at_tile(peer):
        return {"member": m, "lat": lax.shift_right_logical(peer, n_lon.bit_length() - 1), "lon": peer & (n_lon - 1)}

    barrier = pltpu.get_barrier_semaphore()

    def greet_member(d, _):
        pl.semaphore_signal(barrier, inc=1, device_id=at_member(m ^ d), device_id_type=MESH)
        return 0

    def greet_tile(d, _):
        pl.semaphore_signal(barrier, inc=1, device_id=at_tile(t ^ d), device_id_type=MESH)
        return 0

    lax.fori_loop(1, n_mem, greet_member, 0)
    lax.fori_loop(1, tiles, greet_tile, 0)

    loads = [
        pltpu.make_async_copy(theta_hbm.at[:, :, pl.ds(b * LANE, LANE)], th_own.at[b], in_sem.at[4 + b])
        for b in range(blocks)
    ] + [
        pltpu.make_async_copy(
            tracer_hbm, x.at[pl.ds(mem_local, 2), pl.ds(SUB, rows), pl.ds(0, cols)], in_sem.at[1]
        ),
        pltpu.make_async_copy(
            velocity_hbm, x.at[pl.ds(mem_local + 2, 4), pl.ds(SUB, rows), pl.ds(0, cols)], in_sem.at[2]
        ),
    ]
    smalls = [
        pltpu.make_async_copy(src, dst, small_sem.at[i])
        for i, (src, dst) in enumerate(
            ((obs_cell_hbm, obs_cell), (observed_hbm, observed_in), (noise_hbm, noise_in), (perturb_hbm, perturb))
        )
    ]
    for load in loads + smalls:
        load.start()

    for load in loads[:blocks]:
        load.wait()

    def make_kappa(i, _):
        r = pl.multiple_of(i * SUB, SUB)
        for j in range(mem_local):
            for b in range(blocks):
                x[j, pl.ds(r + SUB, SUB), pl.ds(b * LANE, LANE)] = 0.1 * jax.nn.sigmoid(
                    th_own[b, j, pl.ds(r, SUB), :]
                )
        return 0

    lax.fori_loop(0, rows // SUB, make_kappa, 0)
    for load in loads[blocks:]:
        load.wait()

    lane8 = lax.broadcasted_iota(jnp.int32, (SUB, LANE), 1)
    sub8 = lax.broadcasted_iota(jnp.int32, (SUB, LANE), 0)

    def pack(i, _):
        r = pl.multiple_of(i * SUB, SUB)
        east = jnp.zeros((SUB, LANE), F32)
        west = jnp.zeros((SUB, LANE), F32)
        for q in range(planes):
            first = x[q, pl.ds(r + SUB, SUB), pl.ds(0, LANE)]
            last = x[q, pl.ds(r + SUB, SUB), pl.ds(cols - LANE, LANE)]
            east = jnp.where((lane8 // 2) == q, lane_shift(first, 2 * q), east)
            west = jnp.where(((LANE - 1 - lane8) // 2) == q, lane_shift(last, -2 * q), west)
        east_out[pl.ds(r, SUB), :] = east
        west_out[pl.ds(r, SUB), :] = west
        return 0

    lax.fori_loop(0, rows // SUB, pack, 0)

    kept = east_rows.shape[0]
    east_rows[...] = jnp.transpose(east_out[...])[0:kept]
    west_rows[...] = jnp.transpose(west_out[...])[LANE - kept :]

    pl.semaphore_wait(barrier, n_mem - 1 + tiles - 1)

    my_edge = pl.multiple_of((1 - la) * (rows - SUB), SUB)
    their_edge = pl.multiple_of(la * (rows + SUB), SUB)
    lo_w = (lo + n_lon - 1) & (n_lon - 1)
    lo_e = (lo + 1) & (n_lon - 1)

    def halo(i, src, dst, lat, lon):
        return pltpu.make_async_remote_copy(
            src_ref=src, dst_ref=dst, send_sem=halo_send.at[i], recv_sem=halo_recv.at[i],
            device_id={"member": m, "lat": lat, "lon": lon}, device_id_type=MESH,
        )

    halos = [
        halo(0, east_rows, east_got, la, lo_w),
        halo(1, west_rows, west_got, la, lo_e),
        halo(2, east_out.at[pl.ds(my_edge, SUB), :], east_in.at[pl.ds(their_edge, SUB), :], 1 - la, lo_w),
        halo(3, west_out.at[pl.ds(my_edge, SUB), :], west_in.at[pl.ds(their_edge, SUB), :], 1 - la, lo_e),
        halo(4, x.at[:, pl.ds(my_edge + SUB, SUB), pl.ds(0, cols)], lat_in, 1 - la, lo),
    ]
    for copy in halos:
        copy.start()

    far = [0]

    def send_far(count):
        lax.fori_loop(far[0], far[0] + count, start(far_copy), 0)
        far[0] += count

    def e_copy(d):
        peer = p ^ d
        return pltpu.make_async_remote_copy(
            src_ref=e_all.at[p], dst_ref=e_all.at[p], send_sem=e_send.at[peer], recv_sem=e_recv.at[p],
            device_id=at_member(zh * half + peer), device_id_type=MESH,
        )

    def e_arrival(d):
        peer = p ^ d
        return pltpu.make_async_remote_copy(
            src_ref=e_all.at[p], dst_ref=e_all.at[peer], send_sem=e_send.at[peer], recv_sem=e_recv.at[peer],
            device_id=at_member(zh * half + peer), device_id_type=MESH,
        )

    def th_copy(d):
        peer = m ^ d
        r = pl.multiple_of((peer & (half - 1)) * chunk_rows, chunk_rows)
        return pltpu.make_async_remote_copy(
            src_ref=th_own.at[:, :, pl.ds(r, chunk_rows), :],
            dst_ref=th_all.at[:, pl.ds(m * mem_local, mem_local)],
            send_sem=th_send.at[peer], recv_sem=th_recv.at[m],
            device_id=at_member(peer), device_id_type=MESH,
        )

    def th_arrival(d):
        peer = m ^ d
        return pltpu.make_async_remote_copy(
            src_ref=th_own.at[:, :, pl.ds(0, chunk_rows), :],
            dst_ref=th_all.at[:, pl.ds(peer * mem_local, mem_local)],
            send_sem=th_send.at[peer], recv_sem=th_recv.at[peer],
            device_id=at_member(peer), device_id_type=MESH,
        )

    def far_copy(i):
        b, d = i // half, half + (i & (half - 1))
        peer = m ^ d
        r = pl.multiple_of((peer & (half - 1)) * chunk_rows, chunk_rows)
        return pltpu.make_async_remote_copy(
            src_ref=th_own.at[b, :, pl.ds(r, chunk_rows), :],
            dst_ref=th_all.at[b, pl.ds(m * mem_local, mem_local)],
            send_sem=f_send.at[i], recv_sem=f_recv.at[i],
            device_id=at_member(peer), device_id_type=MESH,
        )

    def far_arrival(i):
        b, d = i // half, half + (i & (half - 1))
        peer = m ^ d
        return pltpu.make_async_remote_copy(
            src_ref=th_own.at[b, :, pl.ds(0, chunk_rows), :],
            dst_ref=th_all.at[b, pl.ds(peer * mem_local, mem_local)],
            send_sem=f_send.at[i], recv_sem=f_recv.at[i],
            device_id=at_member(peer), device_id_type=MESH,
        )

    def start(copy):
        def body(d, _):
            copy(d).start()
            return 0
        return body

    def wait_recv(copy):
        def body(d, _):
            copy(d).wait_recv()
            return 0
        return body

    def wait_send(copy):
        def body(d, _):
            copy(d).wait_send()
            return 0
        return body

    lax.fori_loop(1, half, start(th_copy), 0)
    own_chunk = pl.multiple_of(p * chunk_rows, chunk_rows)
    own_th = pltpu.make_async_copy(
        th_own.at[:, :, pl.ds(own_chunk, chunk_rows), :],
        th_all.at[:, pl.ds(m * mem_local, mem_local)],
        in_sem.at[3],
    )
    own_th.start()
    send_far(FAR[0])

    for load in smalls:
        load.wait()

    def row_of(ref):
        return jnp.concatenate([ref[b : b + 1, :] for b in range(obs // LANE)], axis=1)

    observed = row_of(observed_in)
    noise = row_of(noise_in)
    inv_noise = 1.0 / noise
    e_own = observed + jnp.sqrt(noise) * perturb[...]
    e_all[p, 0:mem_local, :] = e_own[:, :obs_half]
    e_all[p, mem_local:SUB, :] = e_own[:, obs_half:]

    for copy in halos:
        copy.wait_recv()
    lax.fori_loop(1, half, start(e_copy), 0)

    send_far(FAR[1])

    unused = jnp.zeros((LANE - kept, rows), F32)
    east_in[pl.ds(SUB, rows), :] = jnp.transpose(jnp.concatenate([east_got[...], unused], axis=0))
    west_in[pl.ds(SUB, rows), :] = jnp.transpose(jnp.concatenate([unused, west_got[...]], axis=0))

    for q in range(planes):
        block = lat_in[q]
        x[q, 0:SUB, 0:cols] = jnp.where(la == 1, block, 0.0)
        x[q, pad_rows - SUB : pad_rows, 0:cols] = jnp.where(la == 0, block, 0.0)

    def unpack(i, _):
        r = pl.multiple_of(i * SUB, SUB)
        inside = ((i > 0) | (la == 1)) & ((i < n_chunks - 1) | (la == 0))
        east = jnp.where(inside, east_in[pl.ds(r, SUB), :], 0.0)
        west = jnp.where(inside, west_in[pl.ds(r, SUB), :], 0.0)
        for q in range(planes):
            x[q, pl.ds(r, SUB), pl.ds(cols, LANE)] = jnp.where(
                lane8 < LANE // 2, lane_shift(east, -2 * q), lane_shift(west, 2 * q)
            )
        return 0

    lax.fori_loop(0, n_chunks, unpack, 0)

    def shared(i, _):
        r = pl.multiple_of(i * SUB, SUB)
        before = pl.multiple_of(jnp.maximum(i - 1, 0) * SUB, SUB)
        after = pl.multiple_of(jnp.minimum(i + 1, n_chunks - 1) * SUB, SUB)
        cur = [x[mem_local + l, pl.ds(r, SUB), :] for l in range(2)]
        for l in range(2):
            c = cur[l]
            u = x[mem_local + 2 + l, pl.ds(r, SUB), :]
            v = x[mem_local + 4 + l, pl.ds(r, SUB), :]
            d_w = lane_shift(c, 1) - c
            d_e = lane_shift(c, -1) - c
            d_s = south_of(x[mem_local + l, pl.ds(before, SUB), :], c) - c
            d_n = north_of(c, x[mem_local + l, pl.ds(after, SUB), :]) - c
            adv = jnp.maximum(u, 0.0) * d_w - jnp.minimum(u, 0.0) * d_e
            adv = adv + jnp.maximum(v, 0.0) * d_s - jnp.minimum(v, 0.0) * d_n
            base[l, pl.ds(r, SUB), :] = c + adv + 0.2 * (cur[1 - l] - c)
            for k, d in enumerate((d_w, d_e, d_s, d_n)):
                diffs[l, k, pl.ds(r, SUB), :] = d
        return 0

    lax.fori_loop(0, n_chunks, shared, 0)
    send_far(FAR[2])

    def first_step(i, _):
        r = pl.multiple_of(i * SUB, SUB)
        before = pl.multiple_of(jnp.maximum(i - 1, 0) * SUB, SUB)
        after = pl.multiple_of(jnp.minimum(i + 1, n_chunks - 1) * SUB, SUB)
        inside = ((i > 0) | (la == 1)) & ((i < n_chunks - 1) | (la == 0))
        for j in range(mem_local):
            k = x[j, pl.ds(r, SUB), :]
            f_e = 0.5 * (k + lane_shift(k, -1))
            f_w = lane_shift(f_e, 1)
            f_s = 0.5 * (k + south_of(x[j, pl.ds(before, SUB), :], k))
            f_n = 0.5 * (k + north_of(k, x[j, pl.ds(after, SUB), :]))
            for n, f in enumerate((f_w, f_e, f_s, f_n)):
                faces[j, n, pl.ds(r, SUB), :] = f
            for l in range(2):
                c = base[l, pl.ds(r, SUB), :]
                for n, f in enumerate((f_w, f_e, f_s, f_n)):
                    c = c + f * diffs[l, n, pl.ds(r, SUB), :]
                c1[j, l, pl.ds(r, SUB), :] = jnp.where(inside, c, 0.0)
        return 0

    lax.fori_loop(0, n_chunks, first_step, 0)
    send_far(FAR[3])

    flat_cells = cells.reshape(rows * blocks * SUB, LANE)

    def second_step(i, _):
        r = pl.multiple_of(i * SUB, SUB)
        before = pl.multiple_of((i - 1) * SUB, SUB)
        after = pl.multiple_of((i + 1) * SUB, SUB)
        u = x[mem_local + 2, pl.ds(r, SUB), pl.ds(0, cols)]
        v = x[mem_local + 4, pl.ds(r, SUB), pl.ds(0, cols)]
        winds = (jnp.maximum(u, 0.0), -jnp.minimum(u, 0.0), jnp.maximum(v, 0.0), -jnp.minimum(v, 0.0))
        for j in range(mem_local):
            wide = c1[j, 0, pl.ds(r, SUB), :]
            c = wide[:, :cols]
            sides = (
                lane_shift(wide, 1)[:, :cols],
                lane_shift(wide, -1)[:, :cols],
                south_of(c1[j, 0, pl.ds(before, SUB), pl.ds(0, cols)], c),
                north_of(c, c1[j, 0, pl.ds(after, SUB), pl.ds(0, cols)]),
            )
            new = c + 0.2 * (c1[j, 1, pl.ds(r, SUB), pl.ds(0, cols)] - c)
            for n in range(4):
                new = new + (winds[n] + faces[j, n, pl.ds(r, SUB), pl.ds(0, cols)]) * (sides[n] - c)
            for b in range(blocks):
                first = ((i - 1) * SUB * blocks + b) * SUB + j
                piece = new[:, b * LANE : (b + 1) * LANE]
                flat_cells[pl.ds(first, SUB, stride=SUB * blocks), :] = piece
                flat_cells[pl.ds(first + mem_local, SUB, stride=SUB * blocks), :] = piece
        return 0

    lax.fori_loop(1, n_chunks - 1, second_step, 0)
    send_far(FAR[4])

    obs_blocks = obs // LANE
    step_of = 8
    low8 = sub8 < mem_local
    obs_lane = [
        jnp.where(
            low8,
            jnp.broadcast_to(obs_cell[a : a + 1, :], (SUB, LANE)),
            jnp.broadcast_to(obs_cell[a + obs_blocks // 2 : a + obs_blocks // 2 + 1, :], (SUB, LANE)),
        )
        & (LANE - 1)
        for a in range(obs_blocks // 2)
    ]

    def gather(i, accs):
        accs = list(accs)
        for k in range(step_of):
            s = i * step_of + k
            here = lane8 == s
            for a in range(obs_blocks // 2):
                got = [
                    cells[lax.shift_right_logical(obs_index[b * LANE + s], LANE.bit_length() - 1)]
                    for b in (a, a + obs_blocks // 2)
                ]
                got = jnp.where(low8, got[0], got[1])
                got = jnp.take_along_axis(got, obs_lane[a], axis=1, mode="promise_in_bounds")
                accs[a] = jnp.where(here, got, accs[a])
        return tuple(accs)

    accs = lax.fori_loop(
        0, LANE // step_of, gather, tuple(jnp.zeros((SUB, LANE), F32) for _ in range(obs_blocks // 2))
    )
    own_pred = jnp.concatenate(accs, axis=1)
    pred_all[m] = own_pred
    pred_out[:, 0:obs_half] = own_pred[0:mem_local]
    pred_out[:, obs_half:obs] = own_pred[mem_local:SUB]

    def p_copy(d):
        peer = m ^ d
        return pltpu.make_async_remote_copy(
            src_ref=pred_all.at[m], dst_ref=pred_all.at[m], send_sem=p_send.at[peer], recv_sem=p_recv.at[m],
            device_id=at_member(peer), device_id_type=MESH,
        )

    def p_arrival(d):
        peer = m ^ d
        return pltpu.make_async_remote_copy(
            src_ref=pred_all.at[m], dst_ref=pred_all.at[peer], send_sem=p_send.at[peer], recv_sem=p_recv.at[peer],
            device_id=at_member(peer), device_id_type=MESH,
        )

    def p_relay(d):
        far_slot = m ^ half
        return pltpu.make_async_remote_copy(
            src_ref=pred_all.at[far_slot], dst_ref=pred_all.at[far_slot],
            send_sem=p_send.at[far_slot ^ d], recv_sem=p_recv.at[far_slot],
            device_id=at_member(m ^ d), device_id_type=MESH,
        )

    p_copy(half).start()
    lax.fori_loop(1, half, start(p_copy), 0)
    send_far(FAR[5])
    lax.fori_loop(1, half, wait_recv(e_arrival), 0)
    p_arrival(half).wait_recv()
    lax.fori_loop(1, half, start(p_relay), 0)
    lax.fori_loop(1, half, wait_recv(p_arrival), 0)
    lax.fori_loop(half + 1, n_mem, wait_recv(p_arrival), 0)

    low = lax.broadcasted_iota(jnp.int32, (SUB, obs_half), 0) < mem_local

    def unfold(a, b):
        top = jnp.where(low, a, pltpu.roll(b, mem_local, axis=0))
        bottom = jnp.where(low, pltpu.roll(a, mem_local, axis=0), b)
        return jnp.concatenate([top, bottom], axis=1)

    def collect(i, total):
        both = unfold(pred_all[2 * i], pred_all[2 * i + 1])
        pred_mat[pl.ds(pl.multiple_of(i * SUB, SUB), SUB), :] = both
        return total + both

    total = lax.fori_loop(0, n_mem // 2, collect, jnp.zeros((SUB, obs), F32))
    mean = jnp.sum(total, axis=0, keepdims=True) * (1.0 / members)

    def center(i, _):
        r = pl.multiple_of(i * SUB, SUB)
        anom = (pred_mat[pl.ds(r, SUB), :] - mean) * scale
        left[pl.ds(r, SUB), :] = anom
        weighted[pl.ds(r, SUB), :] = anom * inv_noise
        return 0

    lax.fori_loop(0, members // SUB, center, 0)

    def innovate(i, _):
        r = pl.multiple_of(zh * half_members + i * SUB, SUB)
        e = unfold(e_all[2 * i], e_all[2 * i + 1])
        left[pl.ds(pl.multiple_of(members + i * SUB, SUB), SUB), :] = e - pred_mat[pl.ds(r, SUB), :]
        return 0

    lax.fori_loop(0, half_members // SUB, innovate, 0)

    g_own[members + half_members :, :] = jnp.zeros((g_rows - members - half_members, members), F32)
    g_own[0 : members + half_members, :] = lax.dot_general(
        left[...], weighted[...], (((1,), (1,)), ((), ())), precision=lax.Precision.HIGHEST,
        preferred_element_type=F32,
    )

    my_part = pl.multiple_of(p * part, SUB)

    def r_copy(d):
        peer = t ^ d
        return pltpu.make_async_remote_copy(
            src_ref=g_own.at[pl.ds(my_part, part), :], dst_ref=rs_in.at[t],
            send_sem=r_send.at[peer], recv_sem=r_recv.at[t],
            device_id=at_tile(peer), device_id_type=MESH,
        )

    def r_arrival(d):
        peer = t ^ d
        return pltpu.make_async_remote_copy(
            src_ref=g_own.at[pl.ds(0, part), :], dst_ref=rs_in.at[peer],
            send_sem=r_send.at[peer], recv_sem=r_recv.at[peer],
            device_id=at_tile(peer), device_id_type=MESH,
        )

    lax.fori_loop(1, tiles, start(r_copy), 0)
    send_far(FAR[6])
    rs_in[t] = g_own[pl.ds(my_part, part), :]
    lax.fori_loop(1, tiles, wait_recv(r_arrival), 0)
    total_part = rs_in[0]
    for k in range(1, tiles):
        total_part = total_part + rs_in[k]
    ab[pl.ds(my_part, part), :] = total_part

    def a_copy(d):
        peer = p ^ d
        mine = ab.at[pl.ds(my_part, part), :]
        return pltpu.make_async_remote_copy(
            src_ref=mine, dst_ref=mine, send_sem=a_send.at[peer], recv_sem=a_recv.at[p],
            device_id=at_member(zh * half + peer), device_id_type=MESH,
        )

    def a_arrival(d):
        peer = p ^ d
        return pltpu.make_async_remote_copy(
            src_ref=ab.at[pl.ds(my_part, part), :],
            dst_ref=ab.at[pl.ds(pl.multiple_of(peer * part, SUB), part), :],
            send_sem=a_send.at[peer], recv_sem=a_recv.at[peer],
            device_id=at_member(zh * half + peer), device_id_type=MESH,
        )

    lax.fori_loop(1, half, start(a_copy), 0)
    send_far(FAR[7])
    lax.fori_loop(1, half, wait_recv(a_arrival), 0)

    send_far(blocks * half - far[0])
    eye = lax.broadcasted_iota(jnp.int32, (members, members), 0) == lax.broadcasted_iota(
        jnp.int32, (members, members), 1
    )
    mat[...] = ab[0:members, :] + jnp.where(eye, LM, 0.0)
    invert(mat)
    w = jnp.dot(
        ab[members : members + half_members, :], mat[...], precision=lax.Precision.HIGHEST,
        preferred_element_type=F32,
    )
    w = scale * (w - jnp.mean(w, axis=1, keepdims=True))
    w_hi = w.astype(BF16)
    w_lo = (w - w_hi.astype(F32)).astype(BF16)
    lhs = jnp.concatenate(
        [jnp.concatenate([w_hi, w_hi], axis=1), jnp.concatenate([w_lo, jnp.zeros_like(w_lo)], axis=1)], axis=0
    )

    own_th.wait()
    lax.fori_loop(1, half, wait_recv(th_arrival), 0)


    def o_copy(b, d):
        peer = p ^ d
        return pltpu.make_async_remote_copy(
            src_ref=upd.at[b, pl.ds(peer * mem_local, mem_local)],
            dst_ref=out_hbm.at[:, pl.ds(own_chunk, chunk_rows), pl.ds(b * LANE, LANE)],
            send_sem=o_send.at[b, peer], recv_sem=o_recv.at[b, p],
            device_id=at_member(zh * half + peer), device_id_type=MESH,
        )

    def o_arrival(b, d):
        peer = p ^ d
        return pltpu.make_async_remote_copy(
            src_ref=upd.at[b, pl.ds(peer * mem_local, mem_local)],
            dst_ref=out_hbm.at[
                :, pl.ds(pl.multiple_of(peer * chunk_rows, chunk_rows), chunk_rows), pl.ds(b * LANE, LANE)
            ],
            send_sem=o_send.at[b, peer], recv_sem=o_recv.at[b, peer],
            device_id=at_member(zh * half + peer), device_id_type=MESH,
        )

    flat = th_all.reshape(blocks * members * chunk_rows, LANE)
    upd_flat = upd.reshape(blocks * half_members * chunk_rows, LANE)
    own_out = []
    for b in range(blocks):
        at_b = b * members * chunk_rows
        lax.fori_loop(b * half, (b + 1) * half, wait_recv(far_arrival), 0)
        for r in range(0, chunk_rows, 2):
            field = jnp.concatenate(
                [flat[pl.ds(at_b + r + k, members, stride=chunk_rows), :] for k in range(2)], axis=1
            )
            hi = field.astype(BF16)
            lo_part = (field - hi.astype(F32)).astype(BF16)
            both = jnp.dot(lhs, jnp.concatenate([hi, lo_part], axis=0), preferred_element_type=F32)
            both = both[:half_members] + both[half_members:]
            for k in range(2):
                own = flat[pl.ds(at_b + zh * (half_members * chunk_rows) + r + k, half_members, stride=chunk_rows), :]
                upd_flat[pl.ds(b * half_members * chunk_rows + r + k, half_members, stride=chunk_rows), :] = (
                    own + both[:, k * LANE : (k + 1) * LANE]
                )
        lax.fori_loop(1, half, start(functools.partial(o_copy, b)), 0)
        own_out.append(
            pltpu.make_async_copy(
                upd.at[b, pl.ds(p * mem_local, mem_local)],
                out_hbm.at[:, pl.ds(own_chunk, chunk_rows), pl.ds(b * LANE, LANE)],
                in_sem.at[4 + b],
            )
        )
        own_out[b].start()

    for copy in halos:
        copy.wait_send()
    lax.fori_loop(1, half, wait_send(e_copy), 0)
    lax.fori_loop(1, half, wait_send(th_copy), 0)
    lax.fori_loop(0, blocks * half, wait_send(far_copy), 0)
    lax.fori_loop(1, half + 1, wait_send(p_copy), 0)
    lax.fori_loop(1, half, wait_send(p_relay), 0)
    lax.fori_loop(1, tiles, wait_send(r_copy), 0)
    lax.fori_loop(1, half, wait_send(a_copy), 0)
    for b in range(blocks):
        own_out[b].wait()
        lax.fori_loop(1, half, wait_recv(functools.partial(o_arrival, b)), 0)
        lax.fori_loop(1, half, wait_send(functools.partial(o_copy, b)), 0)


def on_device(sizes, theta, tracer, velocity, obs_index, observed, noise_var, obs_perturb):
    n_mem, n_lat, n_lon = sizes
    mem_local, rows, cols = theta.shape
    obs = obs_index.shape[0]
    half = n_mem // 2
    tiles = n_lat * n_lon
    members = n_mem * mem_local
    half_members = members // 2
    chunk_rows = rows // half
    planes = mem_local + 6
    pad_rows, pad_cols = rows + 2 * SUB, cols + LANE
    g_rows = half * SUB * -(-(members + half_members) // (half * SUB))
    folded = [a.reshape(obs // LANE, LANE) for a in (obs_index, observed, noise_var)]
    dma = pltpu.SemaphoreType.DMA
    theta_new, pred = pl.pallas_call(
        functools.partial(kernel, sizes),
        out_shape=(
            pltpu.VMEM(theta.shape, F32),
            pltpu.VMEM((mem_local, obs), F32),
        ),
        in_specs=[
            pl.BlockSpec(memory_space=pl.ANY),
            pl.BlockSpec(memory_space=pl.ANY),
            pl.BlockSpec(memory_space=pl.ANY),
            pl.BlockSpec(memory_space=pltpu.SMEM),
            pl.BlockSpec(memory_space=pl.ANY),
            pl.BlockSpec(memory_space=pl.ANY),
            pl.BlockSpec(memory_space=pl.ANY),
            pl.BlockSpec(memory_space=pl.ANY),
        ],
        out_specs=(pl.BlockSpec(memory_space=pl.ANY), pl.BlockSpec(memory_space=pltpu.VMEM)),
        scratch_shapes=[
            pltpu.VMEM((obs // LANE, LANE), jnp.int32),
            pltpu.VMEM((obs // LANE, LANE), F32),
            pltpu.VMEM((obs // LANE, LANE), F32),
            pltpu.VMEM((mem_local, obs), F32),
            pltpu.VMEM((cols // LANE, mem_local, rows, LANE), F32),
            pltpu.VMEM((planes, pad_rows, pad_cols), F32),
            pltpu.VMEM((planes, SUB, cols), F32),
            pltpu.VMEM((rows, LANE), F32),
            pltpu.VMEM((rows, LANE), F32),
            pltpu.VMEM((pad_rows, LANE), F32),
            pltpu.VMEM((pad_rows, LANE), F32),
            pltpu.VMEM((SUB * -(-2 * planes // SUB), rows), F32),
            pltpu.VMEM((SUB * -(-2 * planes // SUB), rows), F32),
            pltpu.VMEM((SUB * -(-2 * planes // SUB), rows), F32),
            pltpu.VMEM((SUB * -(-2 * planes // SUB), rows), F32),
            pltpu.VMEM((2, pad_rows, pad_cols), F32),
            pltpu.VMEM((2, 4, pad_rows, pad_cols), F32),
            pltpu.VMEM((mem_local, 4, pad_rows, pad_cols), F32),
            pltpu.VMEM((mem_local, 2, pad_rows, pad_cols), F32),
            pltpu.VMEM((rows * (cols // LANE), SUB, LANE), F32),
            pltpu.VMEM((cols // LANE, members, chunk_rows, LANE), F32),
            pltpu.VMEM((half, SUB, obs // 2), F32),
            pltpu.VMEM((n_mem, SUB, obs // 2), F32),
            pltpu.VMEM((members, obs), F32),
            pltpu.VMEM((members, obs), F32),
            pltpu.VMEM((members + half_members, obs), F32),
            pltpu.VMEM((g_rows, members), F32),
            pltpu.VMEM((tiles, g_rows // half, members), F32),
            pltpu.VMEM((g_rows, members), F32),
            pltpu.VMEM((members, members), F32),
            pltpu.VMEM((cols // LANE, half_members, chunk_rows, LANE), F32),
            dma((4 + cols // LANE,)),
            dma((4,)),
            dma((5,)), dma((5,)),
            dma((n_mem,)), dma((n_mem,)),
            dma((cols // LANE * half,)), dma((cols // LANE * half,)),
            dma((half,)), dma((half,)),
            dma((n_mem,)), dma((n_mem,)),
            dma((tiles,)), dma((tiles,)),
            dma((half,)), dma((half,)),
            dma((cols // LANE, half)), dma((cols // LANE, half)),
        ],
        compiler_params=pltpu.CompilerParams(
            collective_id=0, has_side_effects=True, vmem_limit_bytes=56 * 1024 * 1024
        ),
        name="inversion",
    )(theta, tracer, velocity.reshape(4, rows, cols), obs_index, *folded, obs_perturb.T)
    return theta_new, pred.T


def solution(mesh):
    placed = (
        P("member", "lat", "lon"),
        P(None, "lat", "lon"),
        P(None, None, "lat", "lon"),
        P(("lat", "lon")),
        P(("lat", "lon")),
        P(("lat", "lon")),
        P(("lat", "lon"), "member"),
    )
    sizes = (mesh.shape["member"], mesh.shape["lat"], mesh.shape["lon"])
    return jax.shard_map(
        functools.partial(on_device, sizes),
        mesh=mesh,
        in_specs=placed,
        out_specs=(P("member", "lat", "lon"), P(("lat", "lon"), "member")),
        check_vma=False,
    )
```
